128 devices in a mesh: grp: 32 (over x, y, core), blk: 4 (over z).
Axes of the slice: x: 4, y: 4, z: 4, core: 2. Of those that a mesh axis runs over, the one named last changes fastest.
Arguments:
- embeddings: bfloat16 [65536, 1024], P(('grp', 'blk'))
- cluster_ids: int32 [65536, 1], P(('grp', 'blk')), may hold values from 0 to 31; in each aligned block of 512 rows (0 to 511, 512 to 1023, ...) at most 64 rows name the same one
- priority: int32 [65536], P(('grp', 'blk')), may hold values from 0 to 65535, each once
Outputs:
- best_match: float32 [65536], P(('grp', 'blk'))
The draws below stay inside these ranges and needn't reach their ends.
Inputs may be any that keep to these rules, and one draw needn't show every extreme that they name: `cluster_ids`: the 512 rows of one device name one cluster at most 64 times, a bound that some block reaches.
All inputs are finite; a program needn't handle non-finite values.
Results may differ from the reference program's by a relative error of at most 0.00049.
Values may be sent and summed in bfloat16 or wider, within the bound.
A program may use at most 128 MiB of HBM per device.

```python
import math
import jax
import jax.numpy as jnp
import numpy as np
from jax import lax

D = 1024
ROW_DEV = 512
SLOT = 64
CLUSTERS = 32
ROWS = 65536
DEVICES = 128


topic_count = 64


def draw_embeddings(key, part):
    key = jax.random.fold_in(key, 7)
    key_topic, key_which, key_power, key_noise = jax.random.split(key, 4)
    topics = jax.random.normal(key_topic, (topic_count, D), jnp.float32)
    which = jax.random.randint(key_which, (ROWS,), 0, topic_count)
    power = jnp.exp(jax.random.uniform(key_power, (ROWS, 1), jnp.float32, math.log(0.3), math.log(3.0)))
    noise = jax.random.normal(key_noise, (ROWS, D), jnp.float32)
    values = noise + power * topics[which]
    return values.astype(jnp.bfloat16)


def assign_block(key, own, number, rows, amount, top, limit, slope):
    ranking = jax.random.permutation(key, amount)
    packed, common = portions_of(amount, rows * top, limit, slope, True), portions_of(amount, rows * top, limit, slope, False)
    places = jnp.arange(amount)

    def named(tallies, offset_by):
        used = int((tallies > 0).sum())
        fixed = max(1, used // 4)
        shifted = fixed + (places - fixed + offset_by * (used - fixed)) % max(1, amount - fixed)
        return jnp.zeros((amount,), jnp.int32).at[ranking[jnp.where(places < fixed, places, shifted)]].set(jnp.asarray(tallies, jnp.int32))

    tallies = jnp.where(number % 4 == 0, named(packed, number // 4), named(common, number - number // 4 - 1))
    mixed = jax.random.permutation(jax.random.fold_in(own, 3), amount)
    giver, sink = mixed[0:amount // 2 * 2:2], mixed[1:amount // 2 * 2:2]
    room = jnp.minimum(tallies[giver] - 1, limit - tallies[sink]) // 2
    room = jnp.where((giver == ranking[0]) | (sink == ranking[0]) | (tallies[sink] == 0), 0, jnp.maximum(room, 0))
    shifted = jax.random.randint(jax.random.fold_in(own, 4), (amount // 2,), 0, 1 << 20) % (room + 1)
    tallies = tallies.at[giver].add(-shifted).at[sink].add(shifted)
    members = jnp.searchsorted(jnp.cumsum(tallies), jnp.arange(rows * top), side="right").astype(jnp.int32)
    table = members.reshape(top, rows).T
    table = table[jax.random.permutation(jax.random.fold_in(own, 1), rows)]
    offset_by = jax.random.randint(jax.random.fold_in(own, 2), (rows, 1), 0, top)
    return jnp.take_along_axis(table, (jnp.arange(top)[None, :] + offset_by) % top, axis=1)


def portions_of(count, total, bound, lean, full):
    weights = [(1 << 20) // math.isqrt(standing ** lean) + 1 for standing in range(1, count + 1)]
    largest = bound if full else min(bound, max(-(-total // count), total * weights[0] // sum(weights)))
    least = 1 if total - largest >= count - 1 else 0
    holding, spare = [largest] + [least] * (count - 1), total - largest - least * (count - 1)
    while spare > 0:
        free = [i for i in range(1, count) if holding[i] < largest] or [i for i in range(1, count) if holding[i] < bound]
        mass, left = sum([weights[i] for i in free]), spare
        for i in free:
            extra = min(bound - holding[i], max(1, left * weights[i] // mass), spare)
            holding[i] = holding[i] + extra
            spare = spare - extra
    return np.array(holding)


def setup_inputs(seed: int = 0) -> dict:
    key_of = jax.random.split(jax.random.key(seed), 4)
    embeddings = draw_embeddings(jax.random.fold_in(key_of[3], 71), 0)
    cluster_ids_keys = jax.random.split(jax.random.fold_in(key_of[1], 1), ROWS // ROW_DEV)
    cluster_ids_turns = jax.random.permutation(jax.random.fold_in(key_of[1], 3), ROWS // ROW_DEV)
    cluster_ids = jax.vmap(lambda own, number: assign_block(jax.random.fold_in(key_of[1], 2), own, number, ROW_DEV, CLUSTERS, 1, SLOT, 2))(cluster_ids_keys, cluster_ids_turns).reshape((ROWS, 1))
    priority = jax.random.permutation(key_of[2], ROWS).astype(jnp.int32)
    return dict(embeddings=embeddings, cluster_ids=cluster_ids, priority=priority)


def reference(embeddings, cluster_ids, priority):
    wide = embeddings.astype(jnp.float32)
    unit = (wide / jnp.sqrt(lax.optimization_barrier(jnp.sum(wide * wide, axis=1, keepdims=True)) + 1e-06)).astype(jnp.bfloat16)
    labels = cluster_ids[:, 0].astype(jnp.int32)
    order = jnp.argsort(labels, stable=True).astype(jnp.int32)
    sorted_unit = unit[order]
    sorted_label = labels[order]
    sorted_rank = priority[order].astype(jnp.int32)
    margin = DEVICES * SLOT
    padded_unit = jnp.pad(sorted_unit, ((margin, margin), (0, 0)))
    padded_label = jnp.pad(sorted_label, (margin, margin), constant_values=-1)
    padded_rank = jnp.pad(sorted_rank, (margin, margin))
    width = ROW_DEV + 2 * margin

    def one_block(index):
        start = (index * ROW_DEV).astype(jnp.int32)
        query = lax.dynamic_slice_in_dim(sorted_unit, start, ROW_DEV, 0)
        q_label = lax.dynamic_slice_in_dim(sorted_label, start, ROW_DEV, 0)
        q_rank = lax.dynamic_slice_in_dim(sorted_rank, start, ROW_DEV, 0)
        keys = lax.dynamic_slice_in_dim(padded_unit, start, width, 0)
        k_label = lax.dynamic_slice_in_dim(padded_label, start, width, 0)
        k_rank = lax.dynamic_slice_in_dim(padded_rank, start, width, 0)
        scores = jnp.dot(query, keys.T, preferred_element_type=jnp.float32)
        allowed = (k_label[None, :] == q_label[:, None]) & (k_rank[None, :] < q_rank[:, None])
        return lax.optimization_barrier(jnp.max(jnp.where(allowed, scores, jnp.float32(-1.0)), axis=1))
    blocks = lax.map(one_block, jnp.arange(DEVICES, dtype=jnp.int32))
    sorted_best = blocks.reshape(-1)
    return jnp.zeros((ROWS,), jnp.float32).at[order].set(sorted_best)
```

```python
import functools

import jax
import jax.numpy as jnp
from jax import lax
from jax.experimental import pallas as pl
from jax.experimental.pallas import tpu as pltpu
from jax.sharding import PartitionSpec as P

MESH = pl.DeviceIdType.MESH
SIDE = 4
CHUNKS = 4
WIDTH = 1024
ROWS = 512
PART = ROWS // CHUNKS
CHIP = 2 * ROWS
STEP = ((1, 0, 0), (-1, 0, 0), (0, 1, 0), (0, -1, 0), (0, 0, 1), (0, 0, -1))

TREE = (
    (0, -1, -1, 0),
    (3, 0, 5, 1),
    (51, 1, 1, 1),
    (4, 0, 2, 1),
    (5, 3, 4, 1),
    (20, 3, 0, 1),
    (12, 0, 3, 1),
    (1, 0, 4, 2),
    (35, 2, 1, 2),
    (23, 5, 5, 2),
    (63, 2, 3, 2),
    (9, 4, 2, 2),
)
SLOTS = len(TREE)
OFFSET = [(v // 16, v // 4 % 4, v % 4) for v, _, _, _ in TREE]

BLOCK_US = 23.0
HOP_US = 0.7
UNIT_US = 1.43
SIBLING_US = 1.5


def difference(p, q):
    return tuple((a - b) % SIDE for a, b in zip(OFFSET[p], OFFSET[q]))


def arrivals():
    start = [0.0] * SLOTS
    for _ in range(SLOTS):
        for n in range(1, SLOTS):
            _, parent, way, wave = TREE[n]
            begin = 0.0 if parent == 0 else start[parent] + BLOCK_US / CHUNKS + HOP_US
            if wave == 2:
                for m in range(1, SLOTS):
                    if TREE[m][2] == way and TREE[m][3] == 1:
                        begin = max(begin, start[m] + BLOCK_US)
            start[n] = begin
    return [
        [0.0 if n == 0 else start[n] + HOP_US + BLOCK_US * (r + 1) / CHUNKS for r in range(CHUNKS)]
        for n in range(SLOTS)
    ]


def make_jobs(ready):
    best = {}
    for s in range(SLOTS):
        for t in range(SLOTS):
            if s == t:
                continue
            d, e = difference(s, t), difference(t, s)
            key = min(d, e)
            if d == e:
                axis = [k for k in range(3) if d[k] == 2][0] + 1
                when = max(ready[s][-1], ready[t][-1])
                jobs = [(when, s, t, 0, axis)]
                cost = 2 * when**3
            else:
                jobs = [
                    (max(ready[s][-1], ready[t][CHUNKS // 2 * (h + 1) - 1]), s, t, h, 0)
                    for h in range(2)
                ]
                cost = sum(j[0] ** 3 for j in jobs)
            if key not in best or cost < best[key][0]:
                best[key] = (cost, jobs)
    assert len(best) == SIDE**3 // 2 + 3
    return sorted(job for _, jobs in best.values() for job in jobs)


def plan():
    ready = arrivals()
    jobs = make_jobs(ready)
    events = sorted((ready[n][r], n, r) for n in range(1, SLOTS) for r in range(CHUNKS))
    steps = []
    seen = set()
    now = 0.0
    first = [[(0.0, 0, 0, 0, 0)] * 2, [(0.0, 0, 0, 1, 0)] * 2]
    queue = list(jobs)
    while queue or first:
        if first:
            mine, first = first, None
        else:
            take = queue[:4]
            queue = queue[4:]
            while len(take) < 4:
                take.append(take[-1])
            mine = [take[0::2], take[1::2]]
        now = max([now] + [j[0] + SIBLING_US for pair in mine for j in pair if j[0] > 0])
        arrived = []
        while events and events[0][0] <= now:
            arrived.append(events.pop(0)[1:])
        steps.append((arrived, mine))
        now += 2 * UNIT_US
    return steps, [e[1:] for e in events]


def kernel(steps, left, x_ref, cluster_ref, rank_ref, out_ref, rows, keys, columns, row_best, col_best, outbox,
           inbox, send, arrive, send_sib, arrive_sib, key_send, key_arrive, key_send_sib, key_arrive_sib,
           back_send, back_arrive):
    grp, z = lax.axis_index("grp"), lax.axis_index("blk")
    x, y, core = grp // (2 * SIDE), grp // 2 % SIDE, grp % 2
    other = 1 - core

    def device(offset, which):
        dx, dy, dz = offset
        return (
            (x + dx + SIDE) % SIDE * (2 * SIDE) + (y + dy + SIDE) % SIDE * 2 + which,
            (z + dz + SIDE) % SIDE,
        )

    neighbours = [device(step, core) for step in STEP]
    sibling = device((0, 0, 0), other)
    children = {n: [m for m in range(1, SLOTS) if TREE[m][1] == n] for n in range(SLOTS)}

    def part(n, r, which):
        return rows.at[n, pl.ds(pl.multiple_of(r * 2 * PART + which * PART, PART), PART)]

    def hop(n, r):
        way = TREE[n][2] ^ 1
        return pltpu.make_async_remote_copy(
            src_ref=part(TREE[n][1], r, core), dst_ref=part(n, r, core), send_sem=send.at[n, r],
            recv_sem=arrive.at[n, r], device_id=neighbours[way], device_id_type=MESH,
        )

    def key_hop(n):
        way = TREE[n][2] ^ 1
        return pltpu.make_async_remote_copy(
            src_ref=keys.at[TREE[n][1], core], dst_ref=keys.at[n, core], send_sem=key_send.at[n],
            recv_sem=key_arrive.at[n], device_id=neighbours[way], device_id_type=MESH,
        )

    def across(n, r):
        return pltpu.make_async_remote_copy(
            src_ref=part(n, r, core), dst_ref=part(n, r, core), send_sem=send_sib.at[n, r],
            recv_sem=arrive_sib.at[n, r], device_id=sibling, device_id_type=MESH,
        )

    def key_across(n):
        return pltpu.make_async_remote_copy(
            src_ref=keys.at[n, core], dst_ref=keys.at[n, core], send_sem=key_send_sib.at[n],
            recv_sem=key_arrive_sib.at[n], device_id=sibling, device_id_type=MESH,
        )

    barrier = pltpu.get_barrier_semaphore()
    for device_id in neighbours + [sibling]:
        pl.semaphore_signal(barrier, inc=1, device_id=device_id, device_id_type=MESH)

    keys[0, core, 0:1, :] = cluster_ref[...].astype(jnp.float32)
    keys[0, core, 1:2, :] = rank_ref[...].astype(jnp.float32)

    def unit(r):
        wide = x_ref[pl.ds(r * PART, PART), :].astype(jnp.float32)
        scale = 1.0 / jnp.sqrt(jnp.sum(wide * wide, axis=1, keepdims=True) + 1e-06)
        rows[0, pl.ds(pl.multiple_of(r * 2 * PART + core * PART, PART), PART), :] = (wide * scale).astype(jnp.bfloat16)

    unit(0)
    pl.semaphore_wait(barrier, len(neighbours) + 1)
    for m in children[0]:
        key_hop(m).start()
    key_across(0).start()
    for r in range(CHUNKS):
        if r:
            unit(r)
        for m in children[0]:
            if TREE[m][3] == 1:
                hop(m, r).start()
        across(0, r).start()
    for m in children[0]:
        if TREE[m][3] == 2:
            for r in range(CHUNKS):
                hop(m, r).start()

    row_best[...] = jnp.full_like(row_best, -1.0)
    col_best[...] = jnp.full_like(col_best, -1.0)

    def columns_of(n):
        for g in range(CHIP // 128):
            r, which = g // 2, g % 2
            for k in range(2):
                line = keys[n, which, k : k + 1, r * PART : (r + 1) * PART]
                columns[left[n], k, g * 128 : (g + 1) * 128, :] = jnp.broadcast_to(line, (128, 128)).T

    def take(n, r):
        if n:
            hop(n, r).wait_recv()
            if r == 0:
                key_hop(n).wait_recv()
                for m in children[n]:
                    key_hop(m).start()
                key_across(n).start()
            for m in children[n]:
                hop(m, r).start()
            across(n, r).start()

    def take_across(n, r):
        across(n, r).wait_recv()
        if r == 0:
            key_across(n).wait_recv()

    bits = [jnp.int32(0), x // 2, y // 2, z // 2]

    def job(code):
        s, t, h, axis = code % 16, code // 16 % 16, code // 256 % 2, code // 512 % 4
        turn = sum((axis == k).astype(jnp.int32) * bits[k] for k in range(1, 4))
        lhs, rhs = s + turn * (t - s), t + turn * (s - t)
        half = h + turn
        own = (s == t).astype(jnp.int32)
        col = rhs + own * (SLOTS - rhs)
        base = pl.multiple_of(half * ROWS, ROWS)
        score = lax.dot_general(
            rows[lhs], rows[rhs, pl.ds(base, ROWS), :], (((1,), (1,)), ((), ())),
            preferred_element_type=jnp.float32,
        )
        return lhs, rhs, half, col, score

    def keep(lhs, rhs, half, col, score):
        cluster, rank = columns[lhs, 0], columns[lhs, 1]
        best = row_best[lhs]
        for q in range(ROWS // 128):
            line = pl.ds(pl.multiple_of((half * 2 + q // 2) * PART, PART), PART)
            cluster_j = keys[rhs, q % 2, 0:1, line]
            rank_j = keys[rhs, q % 2, 1:2, line]
            same = jnp.where(cluster == cluster_j, score[:, q * 128 : (q + 1) * 128], -1.0)
            later = rank > rank_j
            best = jnp.maximum(best, jnp.where(later, same, -1.0))
            back = jnp.max(jnp.where(later, -1.0, same).reshape(CHIP // 8, 8, 128), axis=0)
            lanes = pl.ds(pl.multiple_of(half * ROWS + q * 128, 128), 128)
            col_best[col, :, lanes] = jnp.maximum(col_best[col, :, lanes], back)
        row_best[lhs] = best

    def encode(entry):
        _, s, t, h, axis = entry
        return s + 16 * t + 256 * h + 512 * axis

    firsts = [[encode(jobs[c][0]) for _, jobs in steps] for c in range(2)]
    seconds = [[encode(jobs[c][1]) for _, jobs in steps] for c in range(2)]

    def pick(i, table):
        code = jnp.int32(0)
        for k in range(len(steps)):
            hit = (i == k).astype(jnp.int32)
            code = code + hit * (table[0][k] + core * (table[1][k] - table[0][k]))
        return code

    def body(i, carry):
        done = {0}
        for k, (arrived, jobs) in enumerate(steps):
            new = [s for pair in jobs for _, s, t, _, axis in pair for s in ((s, t) if axis else (s,)) if s not in done]
            new = sorted(set(new))
            done.update(new)
            if arrived or new or k == 0:

                @pl.when(i == k)
                def _(arrived=arrived, new=new, k=k):
                    for n, r in arrived:
                        take(n, r)
                    if k == 0:
                        for r in range(CHUNKS):
                            take_across(0, r)
                        columns_of(0)
                    for n, r in arrived:
                        take_across(n, r)
                    for n in new:
                        columns_of(n)

        one, two = job(pick(i, firsts)), job(pick(i, seconds))
        keep(*one)
        keep(*two)
        return carry

    lax.fori_loop(0, len(steps), body, 0)

    def back(n, which, target):
        return pltpu.make_async_remote_copy(
            src_ref=outbox.at[n, which], dst_ref=inbox.at[n, core], send_sem=back_send.at[n, which],
            recv_sem=back_arrive.at[n, core], device_id=target, device_id_type=MESH,
        )

    def back_wait(n, which):
        pltpu.make_async_remote_copy(
            src_ref=outbox.at[n, which], dst_ref=inbox.at[n, which], send_sem=back_send.at[n, which],
            recv_sem=back_arrive.at[n, which], device_id=sibling, device_id_type=MESH,
        ).wait_recv()

    for n in list(range(1, SLOTS)) + [0]:
        for g in range(CHIP // 128):
            r, which = g // 2, g % 2
            best = jnp.max(col_best[n, :, g * 128 : (g + 1) * 128], axis=0, keepdims=True)
            if n in left:
                mine = row_best[left[n], g * 128 : (g + 1) * 128, :].T
                best = jnp.maximum(best, jnp.max(mine, axis=0, keepdims=True))
            outbox[n, which, r : r + 1, :] = best
        if n:
            for which in range(2):
                back(n, which, device(OFFSET[n], which)).start()
        else:
            back(0, other, sibling).start()

    total = outbox[0, core]
    for n in range(1, SLOTS):
        for which in range(2):
            back_wait(n, which)
            total = jnp.maximum(total, inbox[n, which])
    back_wait(0, other)
    out_ref[...] = jnp.maximum(total, inbox[0, other])

    for n in range(SLOTS):
        for r in range(CHUNKS):
            across(n, r).wait_send()
            if n:
                hop(n, r).wait_send()
        key_across(n).wait_send()
        if n:
            key_hop(n).wait_send()
            for which in range(2):
                back(n, which, sibling).wait_send()
        else:
            back(0, other, sibling).wait_send()


def local(embeddings, cluster_ids, priority):
    steps, late = plan()
    assert not late
    left = sorted({s for _, jobs in steps for pair in jobs for _, s, t, _, axis in pair for s in ((s, t) if axis else (s,))})
    assert left == list(range(len(left)))
    left = {n: n for n in left}
    dma = pltpu.SemaphoreType.DMA
    best = pl.pallas_call(
        functools.partial(kernel, steps, left),
        out_shape=jax.ShapeDtypeStruct((CHUNKS, PART), jnp.float32),
        in_specs=[pl.BlockSpec(memory_space=pltpu.VMEM)] * 3,
        out_specs=pl.BlockSpec(memory_space=pltpu.VMEM),
        scratch_shapes=[
            pltpu.VMEM((SLOTS, CHIP, WIDTH), jnp.bfloat16),
            pltpu.VMEM((SLOTS, 2, 2, ROWS), jnp.float32),
            pltpu.VMEM((len(left), 2, CHIP, 128), jnp.float32),
            pltpu.VMEM((len(left), CHIP, 128), jnp.float32),
            pltpu.VMEM((SLOTS + 1, 8, CHIP), jnp.float32),
            pltpu.VMEM((SLOTS, 2, CHUNKS, PART), jnp.float32),
            pltpu.VMEM((SLOTS, 2, CHUNKS, PART), jnp.float32),
            dma((SLOTS, CHUNKS)),
            dma((SLOTS, CHUNKS)),
            dma((SLOTS, CHUNKS)),
            dma((SLOTS, CHUNKS)),
            dma((SLOTS,)),
            dma((SLOTS,)),
            dma((SLOTS,)),
            dma((SLOTS,)),
            dma((SLOTS, 2)),
            dma((SLOTS, 2)),
        ],
        compiler_params=pltpu.CompilerParams(
            collective_id=0, has_side_effects=True, vmem_limit_bytes=60 * 2**20
        ),
    )(embeddings, cluster_ids.reshape(1, ROWS), priority.reshape(1, ROWS))
    return best.reshape(ROWS)


def solution(mesh):
    placed = (P(("grp", "blk"), None), P(("grp", "blk"), None), P(("grp", "blk")))
    return jax.shard_map(
        local, mesh=mesh, in_specs=placed, out_specs=P(("grp", "blk")), check_vma=False
    )
```

```python
import functools

import jax
import jax.numpy as jnp
from jax import lax
from jax.experimental import pallas as pl
from jax.experimental.pallas import tpu as pltpu
from jax.sharding import PartitionSpec as P

MESH = pl.DeviceIdType.MESH
SIDE = 4
CHUNKS = 4
WIDTH = 1024
ROWS = 512
PART = ROWS // CHUNKS
CHIP = 2 * ROWS
STEP = ((1, 0, 0), (-1, 0, 0), (0, 1, 0), (0, -1, 0), (0, 0, 1), (0, 0, -1))

TREE = (
    (0, -1, -1, 0),
    (3, 0, 5, 1),
    (51, 1, 1, 1),
    (4, 0, 2, 1),
    (5, 3, 4, 1),
    (20, 3, 0, 1),
    (12, 0, 3, 1),
    (1, 0, 4, 2),
    (35, 2, 1, 2),
    (23, 5, 5, 2),
    (63, 2, 3, 2),
    (9, 4, 2, 2),
)
SLOTS = len(TREE)
OFFSET = [(v // 16, v // 4 % 4, v % 4) for v, _, _, _ in TREE]

BLOCK_US = 23.0
HOP_US = 0.7
SIBLING_US = 1.5
LOOP_US = 2.5
EAGER_US = 0.8
SHORT_US = 1.55
LONG_US = 2.65


def arrivals():
    start = [0.0] * SLOTS
    for _ in range(SLOTS):
        for n in range(1, SLOTS):
            _, parent, way, wave = TREE[n]
            begin = 0.0 if parent == 0 else start[parent] + BLOCK_US / CHUNKS + HOP_US
            if wave == 2:
                for m in range(1, SLOTS):
                    if TREE[m][2] == way and TREE[m][3] == 1:
                        begin = max(begin, start[m] + BLOCK_US)
            start[n] = begin
    return [
        [0.0 if n == 0 else start[n] + HOP_US + BLOCK_US * (r + 1) / CHUNKS for r in range(CHUNKS)]
        for n in range(SLOTS)
    ]


def choose(ready):
    best = {}
    for s in range(SLOTS):
        for t in range(SLOTS):
            if s == t:
                continue
            d = tuple((a - b) % SIDE for a, b in zip(OFFSET[s], OFFSET[t]))
            e = tuple(-a % SIDE for a in d)
            axis = [k for k in range(3) if d[k] == 2][0] + 1 if d == e else 0
            if axis:
                times = [max(ready[s][-1], ready[t][-1])] * 2
            else:
                times = [max(ready[s][-1], ready[t][r]) for r in range(CHUNKS)]
            cost = sum(a**3 for a in times) / len(times) + (s > 6) * 1e3
            if min(d, e) not in best or cost < best[min(d, e)][0]:
                best[min(d, e)] = (cost, s, t, axis)
    assert len(best) == SIDE**3 // 2 + 3
    return sorted(best.values())


def plan():
    ready = arrivals()
    events = sorted((ready[n][r], n, r) for n in range(1, SLOTS) for r in range(CHUNKS))
    here = {(0, r): 0.0 for r in range(CHUNKS)}
    crossing = []
    pieces = []
    for _, s, t, axis in choose(ready):
        pieces.append((s, t, axis, set(range(2 if axis else CHUNKS))))
    steps = []
    now = LOOP_US
    ops = []

    def advance(until):
        while True:
            a = events[0][0] if events else 1e9
            b = crossing[0][0] if crossing else 1e9
            if min(a - EAGER_US, b) > until:
                return
            if a - EAGER_US <= b:
                when, n, r = events.pop(0)
                ops.append(("take", n, r))
                crossing.append((max(when, now) + SIBLING_US, n, r))
            else:
                when, n, r = crossing.pop(0)
                ops.append(("cross", n, r))
                here[n, r] = when

    def full(n):
        return all((n, r) in here for r in range(CHUNKS))

    steps.append(([], "short", [(0, 0, 0, 0, 1, 0), (0, 0, 2, 0, 3, 0)]))
    now += SHORT_US
    while pieces:
        advance(now)
        whole = [p for p in pieces if not p[2] and len(p[3]) == CHUNKS and full(p[0]) and full(p[1])]
        ready_pieces = []
        for p in pieces:
            s, t, axis, left = p
            if not full(s):
                continue
            if axis:
                if full(t):
                    ready_pieces.append((p, (0, 1)))
                continue
            if p in whole:
                continue
            ready_pieces += [(p, (r,)) for r in sorted(left) if (t, r) in here]
        shorts = []
        by = {}
        for p, rs in ready_pieces:
            if len(rs) == 2:
                shorts.append([(p, 0), (p, 1)])
            else:
                by.setdefault(p[0], []).append((p, rs[0]))
        single = []
        for s, lst in by.items():
            while len(lst) >= 2:
                shorts.append([lst.pop(0), lst.pop(0)])
            if lst:
                single.append([lst[0], lst[0]])
        last = not events and not crossing
        if len(shorts) < 2 and len(whole) < 2 and last:
            shorts += single
            if len(shorts) < 2 and whole:
                p = whole.pop(0)
                shorts += [[(p, 0), (p, 1)], [(p, 2), (p, 3)]]
            if len(shorts) == 1:
                shorts.append(shorts[0])
        if len(whole) >= 2 and (len(shorts) < 2):
            pair = whole[:2]
            steps.append((ops, "long", [(p[0], p[1]) for p in pair]))
            for p in pair:
                pieces.remove(p)
            ops = []
            now += LONG_US
        elif len(shorts) >= 2:
            entry = []
            for body in shorts[:2]:
                (p, r1), (q, r2) = body
                entry.append((p[0], p[1], r1, q[1], r2, p[2]))
                for a, r in body:
                    a[3].discard(r)
            pieces = [p for p in pieces if p[3]]
            steps.append((ops, "short", entry))
            ops = []
            now += SHORT_US
        else:
            nxt = min([e[0] for e in events[:1]] + [c[0] for c in crossing[:1]])
            now = max(now, nxt)
    assert not events
    while crossing:
        when, n, r = crossing.pop(0)
        ops.append(("cross", n, r))
    return steps, ops, now, ready


def sends(steps):
    waiting, sent = [], set()

    def follow(n, r):
        waiting.extend((m, r) for m in range(1, SLOTS) if TREE[m][1] == n)
        out = []
        for m, q in sorted(waiting, key=lambda a: TREE[a[0]][3]):
            ahead = [w for w in range(1, SLOTS) if TREE[w][2] == TREE[m][2] and TREE[w][3] == 1 and TREE[m][3] == 2]
            if all((w, c) in sent for w in ahead for c in range(CHUNKS)):
                sent.add((m, q))
                waiting.remove((m, q))
                out.append((m, q))
        return out

    first = [follow(0, r) for r in range(CHUNKS)]
    for ops, _, _ in steps:
        for k, op in enumerate(ops):
            if op[0] == "take":
                ops[k] = (*op, follow(op[1], op[2]))
    assert not waiting
    return first


def schedule():
    steps, rest, _, _ = plan()
    last, made = {}, set()
    for k, (_, _, jobs) in enumerate(steps):
        for job in jobs:
            s, others = job[0], (job[1::2] if len(job) == 2 else (job[1], job[3]))
            for n in (s, *others):
                last[n] = k
    out = []
    for k, (ops, kind, jobs) in enumerate(steps):
        ops = list(ops)
        for job in jobs:
            swap = (job[1], job[3]) if len(job) > 2 and job[5] else ()
            for n in (job[0], *swap):
                if n not in made:
                    made.add(n)
                    ops.append(("columns", n))
        ops += [("flush", n) for n in range(SLOTS) if last[n] == k - 1]
        out.append((ops, kind, jobs))
    first = sends(out + [(rest, "", ())])
    return first, out, list(rest) + [("flush", n) for n in range(SLOTS) if last[n] == len(steps) - 1], made


def kernel(first, steps, rest, made, x_ref, cluster_ref, rank_ref, out_ref, rows, keys, columns, row_best, col_best, outbox,
           inbox, send, arrive, send_sib, arrive_sib, key_send, key_arrive, key_send_sib, key_arrive_sib,
           back_send, back_arrive):
    grp, z = lax.axis_index("grp"), lax.axis_index("blk")
    x, y, core = grp // (2 * SIDE), grp // 2 % SIDE, grp % 2
    other = 1 - core

    def device(offset, which):
        dx, dy, dz = offset
        return (
            (x + dx + SIDE) % SIDE * (2 * SIDE) + (y + dy + SIDE) % SIDE * 2 + which,
            (z + dz + SIDE) % SIDE,
        )

    neighbours = [device(step, core) for step in STEP]
    sibling = device((0, 0, 0), other)

    def part(n, r, which):
        return rows.at[n, pl.ds(pl.multiple_of(r * 2 * PART + which * PART, PART), PART)]

    def hop(n, r):
        way = TREE[n][2] ^ 1
        return pltpu.make_async_remote_copy(
            src_ref=part(TREE[n][1], r, core), dst_ref=part(n, r, core), send_sem=send.at[n, r],
            recv_sem=arrive.at[n, r], device_id=neighbours[way], device_id_type=MESH,
        )

    def key_hop(n):
        way = TREE[n][2] ^ 1
        return pltpu.make_async_remote_copy(
            src_ref=keys.at[TREE[n][1], core], dst_ref=keys.at[n, core], send_sem=key_send.at[n],
            recv_sem=key_arrive.at[n], device_id=neighbours[way], device_id_type=MESH,
        )

    def across(n, r):
        return pltpu.make_async_remote_copy(
            src_ref=part(n, r, core), dst_ref=part(n, r, core), send_sem=send_sib.at[n, r],
            recv_sem=arrive_sib.at[n, r], device_id=sibling, device_id_type=MESH,
        )

    def key_across(n):
        return pltpu.make_async_remote_copy(
            src_ref=keys.at[n, core], dst_ref=keys.at[n, core], send_sem=key_send_sib.at[n],
            recv_sem=key_arrive_sib.at[n], device_id=sibling, device_id_type=MESH,
        )

    def forward(pairs):
        for n, r in pairs:
            hop(n, r).start()
            if r == 0:
                key_hop(n).start()

    barrier = pltpu.get_barrier_semaphore()
    for device_id in neighbours + [sibling]:
        pl.semaphore_signal(barrier, inc=1, device_id=device_id, device_id_type=MESH)

    keys[0, core, 0:1, :] = cluster_ref[...].astype(jnp.float32)
    keys[0, core, 1:2, :] = rank_ref[...].astype(jnp.float32)

    def unit(r):
        wide = x_ref[pl.ds(r * PART, PART), :].astype(jnp.float32)
        scale = 1.0 / jnp.sqrt(jnp.sum(wide * wide, axis=1, keepdims=True) + 1e-06)
        rows[0, pl.ds(pl.multiple_of(r * 2 * PART + core * PART, PART), PART), :] = (wide * scale).astype(jnp.bfloat16)

    unit(0)
    pl.semaphore_wait(barrier, len(neighbours) + 1)
    key_across(0).start()
    for r in range(CHUNKS):
        if r:
            unit(r)
        forward(first[r])
        across(0, r).start()

    row_best[...] = jnp.full_like(row_best, -1.0)
    col_best[...] = jnp.full_like(col_best, -1.0)

    def columns_of(n):
        for g in range(CHIP // 128):
            r, which = g // 2, g % 2
            for k in range(2):
                line = keys[n, which, k : k + 1, r * PART : (r + 1) * PART]
                columns[n, k, g * 128 : (g + 1) * 128, :] = jnp.broadcast_to(line, (128, 128)).T

    def take(n, r, follow):
        if r == 0:
            key_hop(n).wait_recv()
        hop(n, r).wait_recv()
        forward(follow)
        if r == 0:
            key_across(n).start()
        across(n, r).start()

    def cross(n, r):
        across(n, r).wait_recv()
        if r == 0:
            key_across(n).wait_recv()

    def back(n, which, target):
        return pltpu.make_async_remote_copy(
            src_ref=outbox.at[n, which], dst_ref=inbox.at[n, core], send_sem=back_send.at[n, which],
            recv_sem=back_arrive.at[n, core], device_id=target, device_id_type=MESH,
        )

    def back_wait(n, which):
        pltpu.make_async_remote_copy(
            src_ref=outbox.at[n, which], dst_ref=inbox.at[n, which], send_sem=back_send.at[n, which],
            recv_sem=back_arrive.at[n, which], device_id=sibling, device_id_type=MESH,
        ).wait_recv()

    def flush(n):
        for g in range(CHIP // 128):
            r, which = g // 2, g % 2
            best = jnp.max(col_best[n, :, g * 128 : (g + 1) * 128], axis=0, keepdims=True)
            if n in made:
                mine = row_best[n, g * 128 : (g + 1) * 128, :].T
                best = jnp.maximum(best, jnp.max(mine, axis=0, keepdims=True))
            outbox[n, which, r : r + 1, :] = best
        if n:
            for which in range(2):
                back(n, which, device(OFFSET[n], which)).start()
        else:
            back(0, other, sibling).start()

    def run(op):
        {"take": take, "cross": cross, "columns": columns_of, "flush": flush}[op[0]](*op[1:])

    bits = [jnp.int32(0), x // 2, y // 2, z // 2]

    def keep(lhs, rhs, col, base, score):
        cluster, rank = columns[lhs, 0], columns[lhs, 1]
        best = row_best[lhs]
        for q in range(score.shape[1] // 128):
            line = pl.ds(pl.multiple_of(base // 2 + q // 2 * PART, PART), PART)
            cluster_j = keys[rhs, q % 2, 0:1, line]
            rank_j = keys[rhs, q % 2, 1:2, line]
            same = jnp.where(cluster == cluster_j, score[:, q * 128 : (q + 1) * 128], -1.0)
            later = rank > rank_j
            best = jnp.maximum(best, jnp.where(later, same, -1.0))
            back = jnp.max(jnp.where(later, -1.0, same).reshape(CHIP // 8, 8, 128), axis=0)
            lanes = pl.ds(pl.multiple_of(base + q * 128, 128), 128)
            col_best[col, :, lanes] = jnp.maximum(col_best[col, :, lanes], back)
        row_best[lhs] = best

    def product(lhs, rhs, base, width):
        return lax.dot_general(
            rows[lhs], rows[rhs, pl.ds(base, width), :], (((1,), (1,)), ((), ())),
            preferred_element_type=jnp.float32,
        )

    def short(code):
        s, t1, r1, t2, r2, axis = (code // d % m for d, m in ((1, 16), (16, 16), (256, 4), (1024, 16), (16384, 4), (65536, 4)))
        turn = sum((axis == k).astype(jnp.int32) * bits[k] for k in range(1, 4))
        lhs = s + turn * (t1 - s)
        todo = []
        for t, r in ((t1, r1), (t2, r2)):
            rhs = t + turn * (s - t)
            base = pl.multiple_of((r + 2 * turn) * 2 * PART, 2 * PART)
            col = rhs + (s == t).astype(jnp.int32) * (SLOTS - rhs)
            todo.append((rhs, col, base, product(lhs, rhs, base, 2 * PART)))
        for rhs, col, base, score in todo:
            keep(lhs, rhs, col, base, score)

    def long(code):
        s, t = code % 16, code // 16 % 16
        keep(s, t, t, 0, product(s, t, 0, CHIP))

    def encode(job):
        scale = (1, 16, 256, 1024, 16384, 65536)
        return sum(a * b for a, b in zip(job, scale))

    def body(i, carry):
        code, wide = jnp.int32(0), jnp.int32(0)
        for k, (ops, kind, jobs) in enumerate(steps):
            one, two = encode(jobs[0]), encode(jobs[1])
            hit = (i == k).astype(jnp.int32)
            code = code + hit * (one + core * (two - one))
            if kind == "long":
                wide = wide + hit
            if ops:

                @pl.when(i == k)
                def _(ops=ops):
                    for op in ops:
                        run(op)

        @pl.when(wide == 0)
        def _():
            short(code)

        @pl.when(wide == 1)
        def _():
            long(code)

        return carry

    for r in range(CHUNKS):
        cross(0, r)
    lax.fori_loop(0, len(steps), body, 0)
    for op in rest:
        run(op)
    for n in range(SLOTS):
        for r in range(CHUNKS):
            across(n, r).wait_send()
            if n:
                hop(n, r).wait_send()
        key_across(n).wait_send()
        if n:
            key_hop(n).wait_send()

    total = outbox[0, core]
    for n in range(1, SLOTS):
        for which in range(2):
            back_wait(n, which)
            total = jnp.maximum(total, inbox[n, which])
    back_wait(0, other)
    out_ref[...] = jnp.maximum(total, inbox[0, other])
    for n in range(1, SLOTS):
        for which in range(2):
            back(n, which, sibling).wait_send()
    back(0, other, sibling).wait_send()


def local(embeddings, cluster_ids, priority):
    first, steps, rest, made = schedule()
    dma = pltpu.SemaphoreType.DMA
    best = pl.pallas_call(
        functools.partial(kernel, first, steps, rest, made),
        out_shape=jax.ShapeDtypeStruct((CHUNKS, PART), jnp.float32),
        in_specs=[pl.BlockSpec(memory_space=pltpu.VMEM)] * 3,
        out_specs=pl.BlockSpec(memory_space=pltpu.VMEM),
        scratch_shapes=[
            pltpu.VMEM((SLOTS, CHIP, WIDTH), jnp.bfloat16),
            pltpu.VMEM((SLOTS, 2, 2, ROWS), jnp.float32),
            pltpu.VMEM((SLOTS, 2, CHIP, 128), jnp.float32),
            pltpu.VMEM((SLOTS, CHIP, 128), jnp.float32),
            pltpu.VMEM((SLOTS + 1, 8, CHIP), jnp.float32),
            pltpu.VMEM((SLOTS, 2, CHUNKS, PART), jnp.float32),
            pltpu.VMEM((SLOTS, 2, CHUNKS, PART), jnp.float32),
            dma((SLOTS, CHUNKS)),
            dma((SLOTS, CHUNKS)),
            dma((SLOTS, CHUNKS)),
            dma((SLOTS, CHUNKS)),
            dma((SLOTS,)),
            dma((SLOTS,)),
            dma((SLOTS,)),
            dma((SLOTS,)),
            dma((SLOTS, 2)),
            dma((SLOTS, 2)),
        ],
        compiler_params=pltpu.CompilerParams(
            collective_id=0, has_side_effects=True, vmem_limit_bytes=60 * 2**20
        ),
    )(embeddings, cluster_ids.reshape(1, ROWS), priority.reshape(1, ROWS))
    return best.reshape(ROWS)


def solution(mesh):
    placed = (P(("grp", "blk"), None), P(("grp", "blk"), None), P(("grp", "blk")))
    return jax.shard_map(
        local, mesh=mesh, in_specs=placed, out_specs=P(("grp", "blk")), check_vma=False
    )
```

```python
import functools

import jax
import jax.numpy as jnp
from jax import lax
from jax.experimental import pallas as pl
from jax.experimental.pallas import tpu as pltpu
from jax.sharding import PartitionSpec as P

MESH = pl.DeviceIdType.MESH
SIDE = 4
CHUNKS = 4
WIDTH = 1024
ROWS = 512
PART = ROWS // CHUNKS
CHIP = 2 * ROWS
STEP = ((1, 0, 0), (-1, 0, 0), (0, 1, 0), (0, -1, 0), (0, 0, 1), (0, 0, -1))

TREE = (
    (0, -1, -1, 0),
    (3, 0, 5, 1),
    (12, 0, 3, 1),
    (16, 0, 0, 1),
    (20, 3, 2, 1),
    (13, 2, 4, 1),
    (48, 0, 1, 1),
    (51, 1, 1, 2),
    (9, 5, 3, 2),
    (50, 7, 5, 2),
    (21, 4, 4, 2),
    (24, 4, 2, 2),
)
SLOTS = len(TREE)
OFFSET = [(v // 16, v // 4 % 4, v % 4) for v, _, _, _ in TREE]

QUARTERS = 4
GROUP = 6
BLOCK_US = 23.0
HOP_US = 0.8
CROSS_US = 1.5
LOOP_US = 2.5
EAGER_US = 0.8
EARLY_US = 12.0
BODY_US = {"short": 1.55, "half": 1.55, "long": 2.65}
OP_US = {"take": 0.15, "cross": 0.06, "columns": 0.35, "flush": 0.3}


def covers(n, r):
    return (2 * r, 2 * r + 1) if TREE[n][3] == 2 else (r,)


def copies(n):
    return 2 if TREE[n][3] == 2 else QUARTERS


def first_on_link(m):
    return [w for w in range(1, SLOTS) if TREE[m][3] == 2 and TREE[w][2] == TREE[m][2] and TREE[w][3] == 1]


def arrivals():
    at = {(0, r): 0.0 for r in range(QUARTERS)}
    free = {}
    for wave in (1, 2):
        todo = [n for n in range(1, SLOTS) if TREE[n][3] == wave]
        for _ in range(SLOTS):
            for n in list(todo):
                parent, way = TREE[n][1], TREE[n][2]
                if parent and (parent, 0) not in at:
                    continue
                clock = max([free.get(way, 0.0)])
                for r in range(copies(n)):
                    need = [c for c in range(copies(parent)) if set(covers(parent, c)) & set(covers(n, r))] if parent else []
                    clock = max([clock] + [at[parent, c] for c in need]) + BLOCK_US / copies(n)
                    at[n, r] = clock + HOP_US
                free[way] = clock
                todo.remove(n)
    return at


def choose(at):
    full = [max(at[n, r] for r in range(copies(n))) for n in range(SLOTS)]
    best = {}
    for s in range(SLOTS):
        for t in range(SLOTS):
            if s == t:
                continue
            d = tuple((a - b) % SIDE for a, b in zip(OFFSET[s], OFFSET[t]))
            e = tuple(-a % SIDE for a in d)
            axis = [k for k in range(3) if d[k] == 2][0] + 1 if d == e else 0
            cost = max(full[s], full[t]), full[s], s
            if min(d, e) not in best or cost < best[min(d, e)][0]:
                best[min(d, e)] = (cost, s, t, axis)
    assert len(best) == SIDE**3 // 2 + 3
    return [b[1:] for b in sorted(best.values())]


def plan():
    at = arrivals()
    events = sorted((when, n, r) for (n, r), when in at.items() if n)
    assert len(at) == QUARTERS + sum(copies(n) for n in range(1, SLOTS))
    crossing = []
    here = {(0, q) for q in range(QUARTERS)}
    todo = [[s, t, axis, None] for s, t, axis in choose(at)]
    steps = [[[], "short", [(0, 0, 0, 0, 1, 0), (0, 0, 2, 0, 3, 0)]]]
    made = {0}
    now = LOOP_US + BODY_US["short"]
    ops = []

    def advance():
        nonlocal now
        while True:
            a = events[0][0] if events else 1e9
            b = crossing[0][0] if crossing else 1e9
            if min(a - EAGER_US, b) > now:
                return
            if a - EAGER_US <= b:
                _, n, r = events.pop(0)
                ops.append(("take", n, r))
                now += OP_US["take"]
                crossing.append((now + CROSS_US, n, r))
            else:
                _, n, r = crossing.pop(0)
                ops.append(("cross", n, r))
                now += OP_US["cross"]
                here.update((n, q) for q in covers(n, r))

    def full(n):
        return all((n, q) in here for q in range(QUARTERS))

    def drained():
        return not events and not crossing

    def half(n, h):
        return (n, 2 * h) in here and (n, 2 * h + 1) in here

    for _ in range(400):
        if not todo:
            break
        advance()
        longs, lone, columns, cells = [], [], {}, {}
        for c in todo:
            s, t, axis, left = c
            if axis:
                if full(s) and full(t):
                    lone.append((c, None, (s, t, 0, t, 1, axis)))
            elif left is None and full(s) and full(t):
                longs.append(c)
            else:
                if full(s) and (left is None and (s == 0 and now < EARLY_US or drained()) or left is not None and left[0] == "short"):
                    for q in range(QUARTERS):
                        if (t, q) in here and (left is None or q in left[1]):
                            columns.setdefault(s, []).append((c, q))
                if left is None and (now < EARLY_US or drained()) or left is not None and left[0] == "half":
                    for a in range(2):
                        for b in range(2):
                            if half(s, a) and half(t, b) and (left is None or (a, b) in left[1]):
                                cells.setdefault((s, a), []).append((c, (a, b)))
        shorts, halves, odd_shorts, odd_halves = [], [], [], []
        for s, found in columns.items():
            for k in range(0, len(found), 2):
                p = found[k : k + 2]
                (odd_shorts if len(p) == 1 else shorts).append(p)
        shorts += lone
        for key, found in cells.items():
            for k in range(0, len(found), 2):
                p = found[k : k + 2]
                (odd_halves if len(p) == 1 else halves).append(p)
        soon = min([e[0] for e in events[:1]] + [c[0] for c in crossing[:1]] + [1e9]) - now
        kind = None
        if len(longs) >= 2:
            kind, entry = "long", [(c[0], c[1]) for c in longs[:2]]
            for c in longs[:2]:
                todo.remove(c)
        elif len(shorts) >= 2 or (len(halves) < 2 and (len(shorts) + len(longs)) and soon > 0.8):
            bodies = shorts[:2]
            if len(bodies) < 2 and longs:
                c = longs[0]
                bodies = bodies + [[(c, 0), (c, 1)], [(c, 2), (c, 3)]]
                bodies = bodies[:2]
            if len(bodies) < 2 and odd_shorts:
                bodies.append(odd_shorts[0] * 2)
            if len(bodies) < 2:
                bodies = bodies * 2
            kind, entry = "short", []
            for body in bodies:
                if isinstance(body, tuple):
                    entry.append(body[2])
                    if body[0] in todo:
                        todo.remove(body[0])
                    continue
                (c, q), (d, p) = body
                entry.append((c[0], c[1], q, d[1], p, 0))
                for e, r in body:
                    if e[3] is None:
                        e[3] = ("short", set(range(QUARTERS)))
                    e[3][1].discard(r)
        elif len(halves) >= 2 or ((halves or odd_halves or odd_shorts) and (drained() or soon > 0.8)):
            if not halves and not odd_halves:
                kind, bodies = "short", (odd_shorts * 2)[:2]
                bodies = [b * 2 for b in bodies]
            else:
                kind, bodies = "half", (halves + [b * 2 for b in odd_halves])[:2]
                bodies = (bodies * 2)[:2]
            entry = []
            for (c, q), (d, p) in bodies:
                if kind == "half":
                    entry.append((c[0], c[1], q[1], d[1], p[1], q[0]))
                else:
                    entry.append((c[0], c[1], q, d[1], p, 0))
                for e, r in ((c, q), (d, p)):
                    if e[3] is None:
                        e[3] = (kind, {(a, b) for a in range(2) for b in range(2)} if kind == "half" else set(range(QUARTERS)))
                    e[3][1].discard(r)
        if kind is None:
            now += max(soon, 0.01)
            continue
        todo = [c for c in todo if c[3] is None or c[3][1]]
        for job in entry:
            lefts = [job[0]] + ([job[1]] if kind == "short" and job[5] else [])
            for n in lefts:
                if n not in made:
                    made.add(n)
                    ops.append(("columns", n))
                    now += OP_US["columns"]
        steps.append([ops, kind, entry])
        ops = []
        now += BODY_US[kind]
    assert not events and not todo
    rest = ops + [("cross", n, r) for _, n, r in crossing]
    last = {}
    for k, (_, _, entry) in enumerate(steps):
        for job in entry:
            for n in (job[0], job[1], *(job[3:4])):
                last[n] = k
    ends = len(steps) - 1
    for n in range(SLOTS):
        if last[n] == ends:
            rest.append(("flush", n))
        else:
            steps[last[n] + 1][0].append(("flush", n))
    return steps, rest, made, now


def sends(steps):
    have, sent = {n: set() for n in range(SLOTS)}, set()

    def follow(n, r):
        have[n].update(covers(n, r))
        out = []
        for m in sorted(range(1, SLOTS), key=lambda k: TREE[k][3]):
            for q in range(copies(m)):
                ahead = {(w, c) for w in first_on_link(m) for c in range(copies(w))}
                if (m, q) not in sent and set(covers(m, q)) <= have[TREE[m][1]] and ahead <= sent:
                    sent.add((m, q))
                    out.append((m, q))
        return out

    first = [follow(0, r) for r in range(QUARTERS)]
    for ops, _, _ in steps:
        for k, op in enumerate(ops):
            if op[0] == "take":
                ops[k] = (*op, follow(op[1], op[2]))
    assert len(sent) == sum(copies(n) for n in range(1, SLOTS))
    return first


def kernel(first, steps, rest, made, x_ref, cluster_ref, rank_ref, out_ref, rows, keys, columns, row_best, col_best, outbox,
           inbox, send, arrive, send_sib, arrive_sib, key_send, key_arrive, key_send_sib, key_arrive_sib,
           back_send, back_arrive):
    grp, z = lax.axis_index("grp"), lax.axis_index("blk")
    x, y, core = grp // (2 * SIDE), grp // 2 % SIDE, grp % 2
    other = 1 - core
    along_x = [lax.rem(x + d, SIDE) * (2 * SIDE) for d in range(SIDE)]
    along_y = [lax.rem(y + d, SIDE) * 2 for d in range(SIDE)]
    along_z = [lax.rem(z + d, SIDE) for d in range(SIDE)]

    def device(offset, which):
        dx, dy, dz = offset
        return along_x[dx % SIDE] + along_y[dy % SIDE] + which, along_z[dz % SIDE]

    neighbours = [device(step, core) for step in STEP]
    sibling = device((0, 0, 0), other)

    def part(n, r, which, slot=None):
        slot = n if slot is None else slot
        if copies(n) == 2:
            return rows.at[slot, pl.ds(2 * r, 2), which]
        return rows.at[slot, r, which]

    def hop(n, r):
        way = TREE[n][2] ^ 1
        return pltpu.make_async_remote_copy(
            src_ref=part(n, r, core, TREE[n][1]), dst_ref=part(n, r, core), send_sem=send.at[n, r],
            recv_sem=arrive.at[n, r], device_id=neighbours[way], device_id_type=MESH,
        )

    def key_hop(n):
        way = TREE[n][2] ^ 1
        return pltpu.make_async_remote_copy(
            src_ref=keys.at[TREE[n][1], core], dst_ref=keys.at[n, core], send_sem=key_send.at[n],
            recv_sem=key_arrive.at[n], device_id=neighbours[way], device_id_type=MESH,
        )

    def across(n, r):
        return pltpu.make_async_remote_copy(
            src_ref=part(n, r, core), dst_ref=part(n, r, core), send_sem=send_sib.at[n, r],
            recv_sem=arrive_sib.at[n, r], device_id=sibling, device_id_type=MESH,
        )

    def key_across(n):
        return pltpu.make_async_remote_copy(
            src_ref=keys.at[n, core], dst_ref=keys.at[n, core], send_sem=key_send_sib.at[n],
            recv_sem=key_arrive_sib.at[n], device_id=sibling, device_id_type=MESH,
        )

    def forward(pairs):
        for n, r in pairs:
            hop(n, r).start()
            if r == 0:
                key_hop(n).start()

    barrier = pltpu.get_barrier_semaphore()
    for device_id in neighbours + [sibling]:
        pl.semaphore_signal(barrier, inc=1, device_id=device_id, device_id_type=MESH)

    keys[0, core, 0:1, :] = cluster_ref[...].astype(jnp.float32)
    keys[0, core, 1:2, :] = rank_ref[...].astype(jnp.float32)

    def unit(r):
        wide = x_ref[pl.ds(r * PART, PART), :].astype(jnp.float32)
        scale = 1.0 / jnp.sqrt(jnp.sum(wide * wide, axis=1, keepdims=True) + 1e-06)
        rows[0, r, core] = (wide * scale).astype(jnp.bfloat16)

    unit(0)
    pl.semaphore_wait(barrier, len(neighbours) + 1)
    key_across(0).start()
    for r in range(CHUNKS):
        if r:
            unit(r)
        forward(first[r])
        across(0, r).start()

    row_best[...] = jnp.full_like(row_best, -1.0)
    col_best[...] = jnp.full_like(col_best, -1.0)

    def columns_of(n):
        for g in range(CHIP // 128):
            r, which = g // 2, g % 2
            for k in range(2):
                line = keys[n, which, k : k + 1, r * PART : (r + 1) * PART]
                columns[n, k, g * 128 : (g + 1) * 128, :] = jnp.broadcast_to(line, (128, 128)).T

    def take(n, r, follow):
        if r == 0:
            key_hop(n).wait_recv()
        hop(n, r).wait_recv()
        forward(follow)
        if r == 0:
            key_across(n).start()
        across(n, r).start()

    def cross(n, r):
        across(n, r).wait_recv()
        if r == 0:
            key_across(n).wait_recv()

    def back(n, which, target):
        return pltpu.make_async_remote_copy(
            src_ref=outbox.at[n, which], dst_ref=inbox.at[n, core], send_sem=back_send.at[n, which],
            recv_sem=back_arrive.at[n, core], device_id=target, device_id_type=MESH,
        )

    def back_wait(n, which):
        pltpu.make_async_remote_copy(
            src_ref=outbox.at[n, which], dst_ref=inbox.at[n, which], send_sem=back_send.at[n, which],
            recv_sem=back_arrive.at[n, which], device_id=sibling, device_id_type=MESH,
        ).wait_recv()

    def flush(n):
        for g in range(CHIP // 128):
            r, which = g // 2, g % 2
            best = jnp.max(col_best[n, :, g * 128 : (g + 1) * 128], axis=0, keepdims=True)
            if n in made:
                mine = row_best[n, g * 128 : (g + 1) * 128, :].T
                best = jnp.maximum(best, jnp.max(mine, axis=0, keepdims=True))
            outbox[n, which, r : r + 1, :] = best
        if n:
            for which in range(2):
                back(n, which, device(OFFSET[n], which)).start()
        else:
            back(0, other, sibling).start()

    def run(op):
        {"take": take, "cross": cross, "columns": columns_of, "flush": flush}[op[0]](*op[1:])

    bits = [jnp.int32(0), x // 2, y // 2, z // 2]

    def keep(lhs, top, rhs, col, base, score):
        lines = pl.ds(top, score.shape[0])
        cluster, rank = columns[lhs, 0, lines, :], columns[lhs, 1, lines, :]
        best = row_best[lhs, lines, :]
        for q in range(score.shape[1] // 128):
            line = pl.ds(pl.multiple_of(base // 2 + q // 2 * PART, PART), PART)
            cluster_j = keys[rhs, q % 2, 0:1, line]
            rank_j = keys[rhs, q % 2, 1:2, line]
            same = jnp.where(cluster == cluster_j, score[:, q * 128 : (q + 1) * 128], -1.0)
            later = rank > rank_j
            best = jnp.maximum(best, jnp.where(later, same, -1.0))
            back = jnp.max(jnp.where(later, -1.0, same).reshape(score.shape[0] // 8, 8, 128), axis=0)
            lanes = pl.ds(pl.multiple_of(base + q * 128, 128), 128)
            col_best[col, :, lanes] = jnp.maximum(col_best[col, :, lanes], back)
        row_best[lhs, lines, :] = best

    def product(lhs, rhs):
        return lax.dot_general(lhs, rhs, (((1,), (1,)), ((), ())), preferred_element_type=jnp.float32)

    def decode(code):
        fields = ((1, 16), (16, 16), (256, 4), (1024, 16), (16384, 4), (65536, 4))
        return (lax.rem(lax.div(code, jnp.int32(d)), jnp.int32(m)) for d, m in fields)

    def short(code):
        s, t1, r1, t2, r2, axis = decode(code)
        turn = sum((axis == k).astype(jnp.int32) * bits[k] for k in range(1, 4))
        lhs = s + turn * (t1 - s)
        todo = []
        for t, r in ((t1, r1), (t2, r2)):
            rhs, at = t + turn * (s - t), r + 2 * turn
            col = rhs + (s == t).astype(jnp.int32) * (SLOTS - rhs)
            score = product(rows[lhs].reshape(CHIP, WIDTH), rows[rhs, at].reshape(2 * PART, WIDTH))
            todo.append((rhs, col, pl.multiple_of(at * 2 * PART, 2 * PART), score))
        for rhs, col, base, score in todo:
            keep(lhs, 0, rhs, col, base, score)

    def half(code):
        s, t1, b1, t2, b2, a = decode(code)
        todo = []
        for t, b in ((t1, b1), (t2, b2)):
            score = product(
                rows[s, pl.ds(2 * a, 2)].reshape(ROWS, WIDTH), rows[t, pl.ds(2 * b, 2)].reshape(ROWS, WIDTH)
            )
            todo.append((t, pl.multiple_of(b * ROWS, ROWS), score))
        for t, base, score in todo:
            keep(s, pl.multiple_of(a * ROWS, ROWS), t, t, base, score)

    def long(code):
        s, t, *_ = decode(code)
        keep(s, 0, t, t, 0, product(rows[s].reshape(CHIP, WIDTH), rows[t].reshape(CHIP, WIDTH)))

    def encode(job):
        scale = (1, 16, 256, 1024, 16384, 65536)
        return sum(a * b for a, b in zip(job, scale))

    codes = []
    for _, _, jobs in steps:
        one, two = encode(jobs[0]), encode(jobs[1])
        codes.append(one + core * (two - one))

    def body(i, carry):
        code, wide = jnp.int32(0), jnp.int32(0)
        for k, (_, kind, _) in enumerate(steps):
            code = jnp.where(i == k, codes[k], code)
            if kind != "short":
                wide = jnp.where(i == k, ("short", "long", "half").index(kind), wide)
        for low in range(0, len(steps), GROUP):
            group = [(k, steps[k][0]) for k in range(low, min(low + GROUP, len(steps))) if steps[k][0]]

            @pl.when((i >= low) & (i < low + GROUP))
            def _(group=group):
                for k, ops in group:

                    @pl.when(i == k)
                    def _(ops=ops):
                        for op in ops:
                            run(op)

        @pl.when(wide == 0)
        def _():
            short(code)

        @pl.when(wide == 1)
        def _():
            long(code)

        @pl.when(wide == 2)
        def _():
            half(code)

        return carry

    for r in range(CHUNKS):
        cross(0, r)
    columns_of(0)
    lax.fori_loop(0, len(steps), body, 0)
    for op in rest:
        run(op)
    for n in range(SLOTS):
        for r in range(copies(n)):
            across(n, r).wait_send()
            if n:
                hop(n, r).wait_send()
        key_across(n).wait_send()
        if n:
            key_hop(n).wait_send()

    total = outbox[0, core]
    for n in range(1, SLOTS):
        for which in range(2):
            back_wait(n, which)
            total = jnp.maximum(total, inbox[n, which])
    back_wait(0, other)
    out_ref[...] = jnp.maximum(total, inbox[0, other])
    for n in range(1, SLOTS):
        for which in range(2):
            back(n, which, sibling).wait_send()
    back(0, other, sibling).wait_send()


def local(embeddings, cluster_ids, priority):
    steps, rest, made, _ = plan()
    first = sends(steps)
    dma = pltpu.SemaphoreType.DMA
    best = pl.pallas_call(
        functools.partial(kernel, first, steps, rest, made),
        out_shape=jax.ShapeDtypeStruct((CHUNKS, PART), jnp.float32),
        in_specs=[pl.BlockSpec(memory_space=pltpu.VMEM)] * 3,
        out_specs=pl.BlockSpec(memory_space=pltpu.VMEM),
        scratch_shapes=[
            pltpu.VMEM((SLOTS, CHUNKS, 2, PART, WIDTH), jnp.bfloat16),
            pltpu.VMEM((SLOTS, 2, 2, ROWS), jnp.float32),
            pltpu.VMEM((SLOTS, 2, CHIP, 128), jnp.float32),
            pltpu.VMEM((SLOTS, CHIP, 128), jnp.float32),
            pltpu.VMEM((SLOTS + 1, 8, CHIP), jnp.float32),
            pltpu.VMEM((SLOTS, 2, CHUNKS, PART), jnp.float32),
            pltpu.VMEM((SLOTS, 2, CHUNKS, PART), jnp.float32),
            dma((SLOTS, CHUNKS)),
            dma((SLOTS, CHUNKS)),
            dma((SLOTS, CHUNKS)),
            dma((SLOTS, CHUNKS)),
            dma((SLOTS,)),
            dma((SLOTS,)),
            dma((SLOTS,)),
            dma((SLOTS,)),
            dma((SLOTS, 2)),
            dma((SLOTS, 2)),
        ],
        compiler_params=pltpu.CompilerParams(
            collective_id=0, has_side_effects=True, vmem_limit_bytes=60 * 2**20
        ),
    )(embeddings, cluster_ids.reshape(1, ROWS), priority.reshape(1, ROWS))
    return best.reshape(ROWS)


def solution(mesh):
    placed = (P(("grp", "blk"), None), P(("grp", "blk"), None), P(("grp", "blk")))
    return jax.shard_map(
        local, mesh=mesh, in_specs=placed, out_specs=P(("grp", "blk")), check_vma=False
    )
```

```python
import functools

import jax
import jax.numpy as jnp
from jax import lax
from jax.experimental import pallas as pl
from jax.experimental.pallas import tpu as pltpu
from jax.sharding import PartitionSpec as P

MESH = pl.DeviceIdType.MESH
SIDE = 4
CHUNKS = 4
WIDTH = 1024
ROWS = 512
PART = ROWS // CHUNKS
CHIP = 2 * ROWS
STEP = ((1, 0, 0), (-1, 0, 0), (0, 1, 0), (0, -1, 0), (0, 0, 1), (0, 0, -1))

TREE = (
    (0, -1, -1, 0),
    (3, 0, 5, 1),
    (12, 0, 3, 1),
    (16, 0, 0, 1),
    (20, 3, 2, 1),
    (13, 2, 4, 1),
    (48, 0, 1, 1),
    (51, 1, 1, 2),
    (9, 5, 3, 2),
    (50, 7, 5, 2),
    (21, 4, 4, 2),
    (24, 4, 2, 2),
)
SLOTS = len(TREE)
OFFSET = [(v // 16, v // 4 % 4, v % 4) for v, _, _, _ in TREE]

QUARTERS = 4
GROUP = 6
BLOCK_US = 23.0
HOP_US = 0.8
CROSS_US = 1.5
LOOP_US = 2.5
EAGER_US = 0.8
EARLY_US = 12.0
BODY_US = {"short": 1.55, "half": 1.55, "long": 2.65}
OP_US = {"take": 0.15, "cross": 0.06, "columns": 0.35, "flush": 0.3}


def covers(n, r):
    return (2 * r, 2 * r + 1) if copies(n) == 2 else (r,)


def copies(n):
    second = [m for m in range(1, SLOTS) if TREE[m][3] == 2]
    chained = TREE[n][1] in second or n in [TREE[m][1] for m in second]
    return 2 if n in second and not chained else QUARTERS


def first_on_link(m):
    return [w for w in range(1, SLOTS) if TREE[m][3] == 2 and TREE[w][2] == TREE[m][2] and TREE[w][3] == 1]


def arrivals():
    at = {(0, r): 0.0 for r in range(QUARTERS)}
    free = {}
    for wave in (1, 2):
        todo = [n for n in range(1, SLOTS) if TREE[n][3] == wave]
        for _ in range(SLOTS):
            for n in list(todo):
                parent, way = TREE[n][1], TREE[n][2]
                if parent and (parent, 0) not in at:
                    continue
                clock = max([free.get(way, 0.0)])
                for r in range(copies(n)):
                    need = [c for c in range(copies(parent)) if set(covers(parent, c)) & set(covers(n, r))] if parent else []
                    clock = max([clock] + [at[parent, c] for c in need]) + BLOCK_US / copies(n)
                    at[n, r] = clock + HOP_US
                free[way] = clock
                todo.remove(n)
    return at


def choose(at):
    full = [max(at[n, r] for r in range(copies(n))) for n in range(SLOTS)]
    best = {}
    for s in range(SLOTS):
        for t in range(SLOTS):
            if s == t:
                continue
            d = tuple((a - b) % SIDE for a, b in zip(OFFSET[s], OFFSET[t]))
            e = tuple(-a % SIDE for a in d)
            axis = [k for k in range(3) if d[k] == 2][0] + 1 if d == e else 0
            cost = max(full[s], full[t]), full[s], s
            if min(d, e) not in best or cost < best[min(d, e)][0]:
                best[min(d, e)] = (cost, s, t, axis)
    assert len(best) == SIDE**3 // 2 + 3
    pairs = [b[1:] for b in sorted(best.values())]
    left = {0} | {n for s, t, axis in pairs if axis for n in (s, t)}
    out = []
    for s, t, axis in pairs:
        if s not in left and t in left:
            s, t = t, s
        left.add(s)
        out.append((s, t, axis))
    return out


def plan():
    at = arrivals()
    events = sorted((when, n, r) for (n, r), when in at.items() if n)
    assert len(at) == QUARTERS + sum(copies(n) for n in range(1, SLOTS))
    crossing = []
    here = {(0, q) for q in range(QUARTERS)}
    todo = [[s, t, axis, None] for s, t, axis in choose(at)]
    steps = [[[], "short", [(0, 0, 0, 0, 1, 0), (0, 0, 2, 0, 3, 0)]]]
    made = {0}
    now = LOOP_US + BODY_US["short"]
    ops = []

    def advance():
        nonlocal now
        while True:
            a = events[0][0] if events else 1e9
            b = crossing[0][0] if crossing else 1e9
            if min(a - EAGER_US, b) > now:
                return
            if a - EAGER_US <= b:
                _, n, r = events.pop(0)
                ops.append(("take", n, r))
                now += OP_US["take"]
                crossing.append((now + CROSS_US, n, r))
            else:
                _, n, r = crossing.pop(0)
                ops.append(("cross", n, r))
                now += OP_US["cross"]
                here.update((n, q) for q in covers(n, r))

    def full(n):
        return all((n, q) in here for q in range(QUARTERS))

    def drained():
        return not events and not crossing

    def half(n, h):
        return (n, 2 * h) in here and (n, 2 * h + 1) in here

    for _ in range(400):
        if not todo:
            break
        advance()
        longs, lone, columns, cells = [], [], {}, {}
        for c in todo:
            s, t, axis, left = c
            if axis:
                if full(s) and full(t):
                    lone.append((c, None, (s, t, 0, t, 1, axis)))
            elif left is None and full(s) and full(t):
                longs.append(c)
            else:
                if full(s) and (left is None and (s == 0 and now < EARLY_US or drained()) or left is not None and left[0] == "short"):
                    for q in range(QUARTERS):
                        if (t, q) in here and (left is None or q in left[1]):
                            columns.setdefault(s, []).append((c, q))
                if left is None and (now < EARLY_US or drained()) or left is not None and left[0] == "half":
                    for a in range(2):
                        for b in range(2):
                            if half(s, a) and half(t, b) and (left is None or (a, b) in left[1]):
                                cells.setdefault((s, a), []).append((c, (a, b)))
        shorts, halves, odd_shorts, odd_halves = [], [], [], []
        for s, found in columns.items():
            for k in range(0, len(found), 2):
                p = found[k : k + 2]
                (odd_shorts if len(p) == 1 else shorts).append(p)
        shorts += lone
        for key, found in cells.items():
            for k in range(0, len(found), 2):
                p = found[k : k + 2]
                (odd_halves if len(p) == 1 else halves).append(p)
        soon = min([e[0] for e in events[:1]] + [c[0] for c in crossing[:1]] + [1e9]) - now
        kind = None
        if len(longs) >= 2:
            kind, entry = "long", [(c[0], c[1]) for c in longs[:2]]
            for c in longs[:2]:
                todo.remove(c)
        elif len(shorts) >= 2 or (len(halves) < 2 and (len(shorts) + len(longs)) and soon > 0.8):
            bodies = shorts[:2]
            if len(bodies) < 2 and longs:
                c = longs[0]
                bodies = bodies + [[(c, 0), (c, 1)], [(c, 2), (c, 3)]]
                bodies = bodies[:2]
            if len(bodies) < 2 and odd_shorts:
                bodies.append(odd_shorts[0] * 2)
            if len(bodies) < 2:
                bodies = bodies * 2
            kind, entry = "short", []
            for body in bodies:
                if isinstance(body, tuple):
                    entry.append(body[2])
                    if body[0] in todo:
                        todo.remove(body[0])
                    continue
                (c, q), (d, p) = body
                entry.append((c[0], c[1], q, d[1], p, 0))
                for e, r in body:
                    if e[3] is None:
                        e[3] = ("short", set(range(QUARTERS)))
                    e[3][1].discard(r)
        elif len(halves) >= 2 or ((halves or odd_halves or odd_shorts) and (drained() or soon > 0.8)):
            if not halves and not odd_halves:
                kind, bodies = "short", (odd_shorts * 2)[:2]
                bodies = [b * 2 for b in bodies]
            else:
                kind, bodies = "half", (halves + [b * 2 for b in odd_halves])[:2]
                bodies = (bodies * 2)[:2]
            entry = []
            for (c, q), (d, p) in bodies:
                if kind == "half":
                    entry.append((c[0], c[1], q[1], d[1], p[1], q[0]))
                else:
                    entry.append((c[0], c[1], q, d[1], p, 0))
                for e, r in ((c, q), (d, p)):
                    if e[3] is None:
                        e[3] = (kind, {(a, b) for a in range(2) for b in range(2)} if kind == "half" else set(range(QUARTERS)))
                    e[3][1].discard(r)
        if kind is None:
            now += max(soon, 0.01)
            continue
        todo = [c for c in todo if c[3] is None or c[3][1]]
        for job in entry:
            lefts = [job[0]] + ([job[1]] if kind == "short" and job[5] else [])
            for n in lefts:
                if n not in made:
                    made.add(n)
                    ops.append(("columns", n))
                    now += OP_US["columns"]
        steps.append([ops, kind, entry])
        ops = []
        now += BODY_US[kind]
    assert not events and not todo
    rest = ops + [("cross", n, r) for _, n, r in crossing]
    last = {}
    for k, (_, _, entry) in enumerate(steps):
        for job in entry:
            for n in (job[0], job[1], *(job[3:4])):
                last[n] = k
    ends = len(steps) - 1
    for n in range(SLOTS):
        if last[n] == ends:
            rest.append(("flush", n))
        else:
            steps[last[n] + 1][0].append(("flush", n))
    return steps, rest, made, now


def sends(steps):
    have, sent = {n: set() for n in range(SLOTS)}, set()

    def follow(n, r):
        have[n].update(covers(n, r))
        out = []
        for m in sorted(range(1, SLOTS), key=lambda k: TREE[k][3]):
            for q in range(copies(m)):
                ahead = {(w, c) for w in first_on_link(m) for c in range(copies(w))}
                if (m, q) not in sent and set(covers(m, q)) <= have[TREE[m][1]] and ahead <= sent:
                    sent.add((m, q))
                    out.append((m, q))
        return out

    first = [follow(0, r) for r in range(QUARTERS)]
    for ops, _, _ in steps:
        for k, op in enumerate(ops):
            if op[0] == "take":
                ops[k] = (*op, follow(op[1], op[2]))
    assert len(sent) == sum(copies(n) for n in range(1, SLOTS))
    return first


def kernel(first, steps, rest, made, x_ref, cluster_ref, rank_ref, out_ref, rows, keys, columns, row_best, col_best, outbox,
           inbox, send, arrive, send_sib, arrive_sib, key_send, key_arrive, key_send_sib, key_arrive_sib,
           back_send, back_arrive, staged, stage):
    grp, z = lax.axis_index("grp"), lax.axis_index("blk")
    x, y, core = grp // (2 * SIDE), grp // 2 % SIDE, grp % 2
    other = 1 - core
    along_x = [lax.rem(x + d, SIDE) * (2 * SIDE) for d in range(SIDE)]
    along_y = [lax.rem(y + d, SIDE) * 2 for d in range(SIDE)]
    along_z = [lax.rem(z + d, SIDE) for d in range(SIDE)]

    def device(offset, which):
        dx, dy, dz = offset
        return along_x[dx % SIDE] + along_y[dy % SIDE] + which, along_z[dz % SIDE]

    neighbours = [device(step, core) for step in STEP]
    sibling = device((0, 0, 0), other)

    def part(n, r, which, slot=None):
        slot = n if slot is None else slot
        if copies(n) == 2:
            return rows.at[slot, pl.ds(2 * r, 2), which]
        return rows.at[slot, r, which]

    def hop(n, r):
        way = TREE[n][2] ^ 1
        return pltpu.make_async_remote_copy(
            src_ref=part(n, r, core, TREE[n][1]), dst_ref=part(n, r, core), send_sem=send.at[n, r],
            recv_sem=arrive.at[n, r], device_id=neighbours[way], device_id_type=MESH,
        )

    def key_hop(n):
        way = TREE[n][2] ^ 1
        return pltpu.make_async_remote_copy(
            src_ref=keys.at[TREE[n][1], core], dst_ref=keys.at[n, core], send_sem=key_send.at[n],
            recv_sem=key_arrive.at[n], device_id=neighbours[way], device_id_type=MESH,
        )

    def across(n, r):
        return pltpu.make_async_remote_copy(
            src_ref=part(n, r, core), dst_ref=part(n, r, core), send_sem=send_sib.at[n, r],
            recv_sem=arrive_sib.at[n, r], device_id=sibling, device_id_type=MESH,
        )

    def key_across(n):
        return pltpu.make_async_remote_copy(
            src_ref=keys.at[n, core], dst_ref=keys.at[n, core], send_sem=key_send_sib.at[n],
            recv_sem=key_arrive_sib.at[n], device_id=sibling, device_id_type=MESH,
        )

    def forward(pairs):
        for n, r in pairs:
            hop(n, r).start()
            if r == 0:
                key_hop(n).start()

    def load(r):
        part_r = pl.ds(r * PART, PART)
        return pltpu.make_async_copy(x_ref.at[part_r], staged.at[part_r], stage.at[r])

    for r in range(CHUNKS):
        load(r).start()
    barrier = pltpu.get_barrier_semaphore()
    for device_id in neighbours + [sibling]:
        pl.semaphore_signal(barrier, inc=1, device_id=device_id, device_id_type=MESH)

    keys[0, core, 0:1, :] = cluster_ref[...].astype(jnp.float32)
    keys[0, core, 1:2, :] = rank_ref[...].astype(jnp.float32)

    def unit(r):
        load(r).wait()
        wide = staged[pl.ds(r * PART, PART), :].astype(jnp.float32)
        scale = 1.0 / jnp.sqrt(jnp.sum(wide * wide, axis=1, keepdims=True) + 1e-06)
        rows[0, r, core] = (wide * scale).astype(jnp.bfloat16)

    row_best[...] = jnp.full_like(row_best, -1.0)
    col_best[...] = jnp.full_like(col_best, -1.0)
    unit(0)
    pl.semaphore_wait(barrier, len(neighbours) + 1)
    key_across(0).start()
    for r in range(CHUNKS):
        if r:
            unit(r)
        forward(first[r])
        across(0, r).start()


    def columns_of(n):
        for g in range(CHIP // 128):
            r, which = g // 2, g % 2
            for k in range(2):
                line = keys[n, which, k : k + 1, r * PART : (r + 1) * PART]
                columns[n, k, g * 128 : (g + 1) * 128, :] = jnp.broadcast_to(line, (128, 128)).T

    def take(n, r, follow):
        if r == 0:
            key_hop(n).wait_recv()
        hop(n, r).wait_recv()
        forward(follow)
        if r == 0:
            key_across(n).start()
        across(n, r).start()

    def cross(n, r):
        across(n, r).wait_recv()
        if r == 0:
            key_across(n).wait_recv()

    def back(n, which, target):
        return pltpu.make_async_remote_copy(
            src_ref=outbox.at[n, which], dst_ref=inbox.at[n, core], send_sem=back_send.at[n, which],
            recv_sem=back_arrive.at[n, core], device_id=target, device_id_type=MESH,
        )

    def back_wait(n, which):
        pltpu.make_async_remote_copy(
            src_ref=outbox.at[n, which], dst_ref=inbox.at[n, which], send_sem=back_send.at[n, which],
            recv_sem=back_arrive.at[n, which], device_id=sibling, device_id_type=MESH,
        ).wait_recv()

    def flush(n):
        for g in range(CHIP // 128):
            r, which = g // 2, g % 2
            best = jnp.max(col_best[n, :, g * 128 : (g + 1) * 128], axis=0, keepdims=True)
            if n in made:
                mine = row_best[n, g * 128 : (g + 1) * 128, :].T
                best = jnp.maximum(best, jnp.max(mine, axis=0, keepdims=True))
            outbox[n, which, r : r + 1, :] = best
        if n:
            for which in range(2):
                back(n, which, device(OFFSET[n], which)).start()
        else:
            back(0, other, sibling).start()

    def run(op):
        {"take": take, "cross": cross, "columns": columns_of, "flush": flush}[op[0]](*op[1:])

    bits = [jnp.int32(0), x // 2, y // 2, z // 2]

    def keep(lhs, top, rhs, col, base, score):
        lines = pl.ds(top, score.shape[0])
        cluster, rank = columns[lhs, 0, lines, :], columns[lhs, 1, lines, :]
        best = row_best[lhs, lines, :]
        for q in range(score.shape[1] // 128):
            line = pl.ds(pl.multiple_of(base // 2 + q // 2 * PART, PART), PART)
            cluster_j = keys[rhs, q % 2, 0:1, line]
            rank_j = keys[rhs, q % 2, 1:2, line]
            same = jnp.where(cluster == cluster_j, score[:, q * 128 : (q + 1) * 128], -1.0)
            later = rank > rank_j
            best = jnp.maximum(best, jnp.where(later, same, -1.0))
            back = jnp.max(jnp.where(later, -1.0, same).reshape(score.shape[0] // 8, 8, 128), axis=0)
            lanes = pl.ds(pl.multiple_of(base + q * 128, 128), 128)
            col_best[col, :, lanes] = jnp.maximum(col_best[col, :, lanes], back)
        row_best[lhs, lines, :] = best

    def product(lhs, rhs):
        return lax.dot_general(lhs, rhs, (((1,), (1,)), ((), ())), preferred_element_type=jnp.float32)

    def decode(code):
        fields = ((1, 16), (16, 16), (256, 4), (1024, 16), (16384, 4), (65536, 4))
        return (lax.rem(lax.div(code, jnp.int32(d)), jnp.int32(m)) for d, m in fields)

    def short(code):
        s, t1, r1, t2, r2, axis = decode(code)
        turn = sum((axis == k).astype(jnp.int32) * bits[k] for k in range(1, 4))
        lhs = s + turn * (t1 - s)
        todo = []
        for t, r in ((t1, r1), (t2, r2)):
            rhs, at = t + turn * (s - t), r + 2 * turn
            col = rhs + (s == t).astype(jnp.int32) * (SLOTS - rhs)
            score = product(rows[lhs].reshape(CHIP, WIDTH), rows[rhs, at].reshape(2 * PART, WIDTH))
            todo.append((rhs, col, pl.multiple_of(at * 2 * PART, 2 * PART), score))
        for rhs, col, base, score in todo:
            keep(lhs, 0, rhs, col, base, score)

    def half(code):
        s, t1, b1, t2, b2, a = decode(code)
        todo = []
        for t, b in ((t1, b1), (t2, b2)):
            score = product(
                rows[s, pl.ds(2 * a, 2)].reshape(ROWS, WIDTH), rows[t, pl.ds(2 * b, 2)].reshape(ROWS, WIDTH)
            )
            todo.append((t, pl.multiple_of(b * ROWS, ROWS), score))
        for t, base, score in todo:
            keep(s, pl.multiple_of(a * ROWS, ROWS), t, t, base, score)

    def long(code):
        s, t, *_ = decode(code)
        keep(s, 0, t, t, 0, product(rows[s].reshape(CHIP, WIDTH), rows[t].reshape(CHIP, WIDTH)))

    def encode(job):
        scale = (1, 16, 256, 1024, 16384, 65536)
        return sum(a * b for a, b in zip(job, scale))

    codes = []
    for _, _, jobs in steps:
        one, two = encode(jobs[0]), encode(jobs[1])
        codes.append(one + core * (two - one))

    def body(i, carry):
        code, wide = jnp.int32(0), jnp.int32(0)
        for k, (_, kind, _) in enumerate(steps):
            code = jnp.where(i == k, codes[k], code)
            if kind != "short":
                wide = jnp.where(i == k, ("short", "long", "half").index(kind), wide)
        for low in range(0, len(steps), GROUP):
            group = [(k, steps[k][0]) for k in range(low, min(low + GROUP, len(steps))) if steps[k][0]]

            @pl.when((i >= low) & (i < low + GROUP))
            def _(group=group):
                for k, ops in group:

                    @pl.when(i == k)
                    def _(ops=ops):
                        for op in ops:
                            run(op)

        @pl.when(wide == 0)
        def _():
            short(code)

        @pl.when(wide == 1)
        def _():
            long(code)

        @pl.when(wide == 2)
        def _():
            half(code)

        return carry

    for r in range(CHUNKS):
        cross(0, r)
    columns_of(0)
    lax.fori_loop(0, len(steps), body, 0)
    for op in rest:
        run(op)
    for n in range(SLOTS):
        for r in range(copies(n)):
            across(n, r).wait_send()
            if n:
                hop(n, r).wait_send()
        key_across(n).wait_send()
        if n:
            key_hop(n).wait_send()

    total = outbox[0, core]
    for n in range(1, SLOTS):
        for which in range(2):
            back_wait(n, which)
            total = jnp.maximum(total, inbox[n, which])
    back_wait(0, other)
    out_ref[...] = jnp.maximum(total, inbox[0, other])
    for n in range(1, SLOTS):
        for which in range(2):
            back(n, which, sibling).wait_send()
    back(0, other, sibling).wait_send()


def local(embeddings, cluster_ids, priority):
    steps, rest, made, _ = plan()
    first = sends(steps)
    dma = pltpu.SemaphoreType.DMA
    best = pl.pallas_call(
        functools.partial(kernel, first, steps, rest, made),
        out_shape=jax.ShapeDtypeStruct((CHUNKS, PART), jnp.float32),
        in_specs=[pl.BlockSpec(memory_space=pl.ANY)] + [pl.BlockSpec(memory_space=pltpu.VMEM)] * 2,
        out_specs=pl.BlockSpec(memory_space=pltpu.VMEM),
        scratch_shapes=[
            pltpu.VMEM((SLOTS, CHUNKS, 2, PART, WIDTH), jnp.bfloat16),
            pltpu.VMEM((SLOTS, 2, 2, ROWS), jnp.float32),
            pltpu.VMEM((SLOTS, 2, CHIP, 128), jnp.float32),
            pltpu.VMEM((SLOTS, CHIP, 128), jnp.float32),
            pltpu.VMEM((SLOTS + 1, 8, CHIP), jnp.float32),
            pltpu.VMEM((SLOTS, 2, CHUNKS, PART), jnp.float32),
            pltpu.VMEM((SLOTS, 2, CHUNKS, PART), jnp.float32),
            dma((SLOTS, CHUNKS)),
            dma((SLOTS, CHUNKS)),
            dma((SLOTS, CHUNKS)),
            dma((SLOTS, CHUNKS)),
            dma((SLOTS,)),
            dma((SLOTS,)),
            dma((SLOTS,)),
            dma((SLOTS,)),
            dma((SLOTS, 2)),
            dma((SLOTS, 2)),
            pltpu.VMEM((ROWS, WIDTH), jnp.bfloat16),
            dma((CHUNKS,)),
        ],
        compiler_params=pltpu.CompilerParams(
            collective_id=0, has_side_effects=True, vmem_limit_bytes=60 * 2**20
        ),
    )(embeddings, cluster_ids.reshape(1, ROWS), priority.reshape(1, ROWS))
    return best.reshape(ROWS)


def solution(mesh):
    placed = (P(("grp", "blk"), None), P(("grp", "blk"), None), P(("grp", "blk")))
    return jax.shard_map(
        local, mesh=mesh, in_specs=placed, out_specs=P(("grp", "blk")), check_vma=False
    )
```

```python
import functools

import jax
import jax.numpy as jnp
from jax import lax
from jax.experimental import pallas as pl
from jax.experimental.pallas import tpu as pltpu
from jax.sharding import PartitionSpec as P

MESH = pl.DeviceIdType.MESH
SIDE = 4
CHUNKS = 4
WIDTH = 1024
ROWS = 512
PART = ROWS // CHUNKS
CHIP = 2 * ROWS
STEP = ((1, 0, 0), (-1, 0, 0), (0, 1, 0), (0, -1, 0), (0, 0, 1), (0, 0, -1))

TREE = (
    (0, -1, -1, 0),
    (3, 0, 5, 1),
    (12, 0, 3, 1),
    (16, 0, 0, 1),
    (20, 3, 2, 1),
    (13, 2, 4, 1),
    (48, 0, 1, 1),
    (51, 1, 1, 2),
    (9, 5, 3, 2),
    (50, 7, 5, 2),
    (21, 4, 4, 2),
    (24, 4, 2, 2),
)
SLOTS = len(TREE)
OFFSET = [(v // 16, v // 4 % 4, v % 4) for v, _, _, _ in TREE]

QUARTERS = 4
GROUP = 6
BLOCK_US = 23.0
HOP_US = 0.8
CROSS_US = 1.5
LOOP_US = 2.5
EAGER_US = 0.8
EARLY_US = 12.0
BODY_US = {"short": 1.55, "half": 1.55, "long": 2.65}
OP_US = {"take": 0.15, "cross": 0.06, "columns": 0.35, "flush": 0.3}


def covers(n, r):
    return (2 * r, 2 * r + 1) if copies(n) == 2 else (r,)


def copies(n):
    second = [m for m in range(1, SLOTS) if TREE[m][3] == 2]
    chained = TREE[n][1] in second or n in [TREE[m][1] for m in second]
    return 2 if n in second and not chained else QUARTERS


def first_on_link(m):
    return [w for w in range(1, SLOTS) if TREE[m][3] == 2 and TREE[w][2] == TREE[m][2] and TREE[w][3] == 1]


def arrivals():
    at = {(0, r): 0.0 for r in range(QUARTERS)}
    free = {}
    for wave in (1, 2):
        todo = [n for n in range(1, SLOTS) if TREE[n][3] == wave]
        for _ in range(SLOTS):
            for n in list(todo):
                parent, way = TREE[n][1], TREE[n][2]
                if parent and (parent, 0) not in at:
                    continue
                clock = max([free.get(way, 0.0)])
                for r in range(copies(n)):
                    need = [c for c in range(copies(parent)) if set(covers(parent, c)) & set(covers(n, r))] if parent else []
                    clock = max([clock] + [at[parent, c] for c in need]) + BLOCK_US / copies(n)
                    at[n, r] = clock + HOP_US
                free[way] = clock
                todo.remove(n)
    return at


def choose(at):
    full = [max(at[n, r] for r in range(copies(n))) for n in range(SLOTS)]
    best = {}
    for s in range(SLOTS):
        for t in range(SLOTS):
            if s == t:
                continue
            d = tuple((a - b) % SIDE for a, b in zip(OFFSET[s], OFFSET[t]))
            e = tuple(-a % SIDE for a in d)
            axis = [k for k in range(3) if d[k] == 2][0] + 1 if d == e else 0
            cost = max(full[s], full[t]), full[s], s
            if min(d, e) not in best or cost < best[min(d, e)][0]:
                best[min(d, e)] = (cost, s, t, axis)
    assert len(best) == SIDE**3 // 2 + 3
    pairs = [b[1:] for b in sorted(best.values())]
    left = {0} | {n for s, t, axis in pairs if axis for n in (s, t)}
    out = []
    for s, t, axis in pairs:
        if s not in left and t in left:
            s, t = t, s
        left.add(s)
        out.append((s, t, axis))
    return out


def plan():
    at = arrivals()
    events = sorted((when, n, r) for (n, r), when in at.items() if n)
    assert len(at) == QUARTERS + sum(copies(n) for n in range(1, SLOTS))
    crossing = []
    here = {(0, q) for q in range(QUARTERS)}
    todo = [[s, t, axis, None] for s, t, axis in choose(at)]
    steps = [[[], "short", [(0, 0, 0, 0, 1, 0), (0, 0, 2, 0, 3, 0)]]]
    made = {0}
    now = LOOP_US + BODY_US["short"]
    ops = []

    def advance():
        nonlocal now
        while True:
            a = events[0][0] if events else 1e9
            b = crossing[0][0] if crossing else 1e9
            if min(a - EAGER_US, b) > now:
                return
            if a - EAGER_US <= b:
                _, n, r = events.pop(0)
                ops.append(("take", n, r))
                now += OP_US["take"]
                crossing.append((now + CROSS_US, n, r))
            else:
                _, n, r = crossing.pop(0)
                ops.append(("cross", n, r))
                now += OP_US["cross"]
                here.update((n, q) for q in covers(n, r))

    def full(n):
        return all((n, q) in here for q in range(QUARTERS))

    def drained():
        return not events and not crossing

    def half(n, h):
        return (n, 2 * h) in here and (n, 2 * h + 1) in here

    for _ in range(400):
        if not todo:
            break
        advance()
        longs, lone, columns, cells = [], [], {}, {}
        for c in todo:
            s, t, axis, left = c
            if axis:
                if full(s) and full(t):
                    lone.append((c, None, (s, t, 0, t, 1, axis)))
            elif left is None and full(s) and full(t):
                longs.append(c)
            else:
                if full(s) and (left is None and (s == 0 and now < EARLY_US or drained()) or left is not None and left[0] == "short"):
                    for q in range(QUARTERS):
                        if (t, q) in here and (left is None or q in left[1]):
                            columns.setdefault(s, []).append((c, q))
                if left is None and (now < EARLY_US or drained()) or left is not None and left[0] == "half":
                    for a in range(2):
                        for b in range(2):
                            if half(s, a) and half(t, b) and (left is None or (a, b) in left[1]):
                                cells.setdefault((s, a), []).append((c, (a, b)))
        shorts, halves, odd_shorts, odd_halves = [], [], [], []
        for s, found in columns.items():
            for k in range(0, len(found), 2):
                p = found[k : k + 2]
                (odd_shorts if len(p) == 1 else shorts).append(p)
        shorts += lone
        for key, found in cells.items():
            for k in range(0, len(found), 2):
                p = found[k : k + 2]
                (odd_halves if len(p) == 1 else halves).append(p)
        soon = min([e[0] for e in events[:1]] + [c[0] for c in crossing[:1]] + [1e9]) - now
        kind = None
        if len(longs) >= 2:
            kind, entry = "long", [(c[0], c[1]) for c in longs[:2]]
            for c in longs[:2]:
                todo.remove(c)
        elif len(shorts) >= 2 or (len(halves) < 2 and (len(shorts) + len(longs)) and soon > 0.8):
            bodies = shorts[:2]
            if len(bodies) < 2 and longs:
                c = longs[0]
                bodies = bodies + [[(c, 0), (c, 1)], [(c, 2), (c, 3)]]
                bodies = bodies[:2]
            if len(bodies) < 2 and odd_shorts:
                bodies.append(odd_shorts[0] * 2)
            if len(bodies) < 2:
                bodies = bodies * 2
            kind, entry = "short", []
            for body in bodies:
                if isinstance(body, tuple):
                    entry.append(body[2])
                    if body[0] in todo:
                        todo.remove(body[0])
                    continue
                (c, q), (d, p) = body
                entry.append((c[0], c[1], q, d[1], p, 0))
                for e, r in body:
                    if e[3] is None:
                        e[3] = ("short", set(range(QUARTERS)))
                    e[3][1].discard(r)
        elif len(halves) >= 2 or ((halves or odd_halves or odd_shorts) and (drained() or soon > 0.8)):
            if not halves and not odd_halves:
                kind, bodies = "short", (odd_shorts * 2)[:2]
                bodies = [b * 2 for b in bodies]
            else:
                kind, bodies = "half", (halves + [b * 2 for b in odd_halves])[:2]
                bodies = (bodies * 2)[:2]
            entry = []
            for (c, q), (d, p) in bodies:
                if kind == "half":
                    entry.append((c[0], c[1], q[1], d[1], p[1], q[0]))
                else:
                    entry.append((c[0], c[1], q, d[1], p, 0))
                for e, r in ((c, q), (d, p)):
                    if e[3] is None:
                        e[3] = (kind, {(a, b) for a in range(2) for b in range(2)} if kind == "half" else set(range(QUARTERS)))
                    e[3][1].discard(r)
        if kind is None:
            now += max(soon, 0.01)
            continue
        todo = [c for c in todo if c[3] is None or c[3][1]]
        for job in entry:
            lefts = [job[0]] + ([job[1]] if kind == "short" and job[5] else [])
            for n in lefts:
                if n not in made:
                    made.add(n)
                    ops.append(("columns", n))
                    now += OP_US["columns"]
        steps.append([ops, kind, entry])
        ops = []
        now += BODY_US[kind]
    assert not events and not todo
    rest = ops + [("cross", n, r) for _, n, r in crossing]
    last = {}
    for k, (_, _, entry) in enumerate(steps):
        for job in entry:
            for n in (job[0], job[1], *(job[3:4])):
                last[n] = k
    ends = len(steps) - 1
    for n in range(SLOTS):
        if last[n] == ends:
            rest.append(("flush", n))
        else:
            steps[last[n] + 1][0].append(("flush", n))
    return steps, rest, made, now


def sends(steps):
    have, sent = {n: set() for n in range(SLOTS)}, set()

    def follow(n, r):
        have[n].update(covers(n, r))
        out = []
        for m in sorted(range(1, SLOTS), key=lambda k: TREE[k][3]):
            for q in range(copies(m)):
                ahead = {(w, c) for w in first_on_link(m) for c in range(copies(w))}
                if (m, q) not in sent and set(covers(m, q)) <= have[TREE[m][1]] and ahead <= sent:
                    sent.add((m, q))
                    out.append((m, q))
        return out

    first = [follow(0, r) for r in range(QUARTERS)]
    for ops, _, _ in steps:
        for k, op in enumerate(ops):
            if op[0] == "take":
                ops[k] = (*op, follow(op[1], op[2]))
    assert len(sent) == sum(copies(n) for n in range(1, SLOTS))
    return first


def kernel(first, steps, rest, made, x_ref, cluster_ref, rank_ref, out_ref, rows, keys, columns, row_best, col_best, outbox,
           inbox, send, arrive, send_sib, arrive_sib, key_send, key_arrive, key_send_sib, key_arrive_sib,
           back_send, back_arrive, staged, stage):
    grp, z = lax.axis_index("grp"), lax.axis_index("blk")
    x, y, core = grp // (2 * SIDE), grp // 2 % SIDE, grp % 2
    other = 1 - core
    along_x = [lax.rem(x + d, SIDE) * (2 * SIDE) for d in range(SIDE)]
    along_y = [lax.rem(y + d, SIDE) * 2 for d in range(SIDE)]
    along_z = [lax.rem(z + d, SIDE) for d in range(SIDE)]

    def device(offset, which):
        dx, dy, dz = offset
        return along_x[dx % SIDE] + along_y[dy % SIDE] + which, along_z[dz % SIDE]

    neighbours = [device(step, core) for step in STEP]
    sibling = device((0, 0, 0), other)

    def part(n, r, which, slot=None):
        slot = n if slot is None else slot
        if copies(n) == 2:
            return rows.at[slot, pl.ds(2 * r, 2), which]
        return rows.at[slot, r, which]

    def hop(n, r):
        way = TREE[n][2] ^ 1
        return pltpu.make_async_remote_copy(
            src_ref=part(n, r, core, TREE[n][1]), dst_ref=part(n, r, core), send_sem=send.at[n, r],
            recv_sem=arrive.at[n, r], device_id=neighbours[way], device_id_type=MESH,
        )

    def key_hop(n):
        way = TREE[n][2] ^ 1
        return pltpu.make_async_remote_copy(
            src_ref=keys.at[TREE[n][1], core], dst_ref=keys.at[n, core], send_sem=key_send.at[n],
            recv_sem=key_arrive.at[n], device_id=neighbours[way], device_id_type=MESH,
        )

    def across(n, r):
        return pltpu.make_async_remote_copy(
            src_ref=part(n, r, core), dst_ref=part(n, r, core), send_sem=send_sib.at[n, r],
            recv_sem=arrive_sib.at[n, r], device_id=sibling, device_id_type=MESH,
        )

    def key_across(n):
        return pltpu.make_async_remote_copy(
            src_ref=keys.at[n, core], dst_ref=keys.at[n, core], send_sem=key_send_sib.at[n],
            recv_sem=key_arrive_sib.at[n], device_id=sibling, device_id_type=MESH,
        )

    def forward(pairs):
        for n, r in pairs:
            hop(n, r).start()
            if r == 0:
                key_hop(n).start()

    def load(r):
        part_r = pl.ds(r * PART, PART)
        return pltpu.make_async_copy(x_ref.at[part_r], staged.at[part_r], stage.at[r])

    for r in range(CHUNKS):
        load(r).start()
    barrier = pltpu.get_barrier_semaphore()
    for device_id in neighbours + [sibling]:
        pl.semaphore_signal(barrier, inc=1, device_id=device_id, device_id_type=MESH)

    keys[0, core, 0:1, :] = cluster_ref[...].astype(jnp.float32)
    keys[0, core, 1:2, :] = rank_ref[...].astype(jnp.float32)

    def unit(r):
        load(r).wait()
        wide = staged[pl.ds(r * PART, PART), :].astype(jnp.float32)
        scale = 1.0 / jnp.sqrt(jnp.sum(wide * wide, axis=1, keepdims=True) + 1e-06)
        rows[0, r, core] = (wide * scale).astype(jnp.bfloat16)

    row_best[...] = jnp.full_like(row_best, -1.0)
    col_best[...] = jnp.full_like(col_best, -1.0)
    unit(0)
    pl.semaphore_wait(barrier, len(neighbours) + 1)
    key_across(0).start()
    for r in range(CHUNKS):
        if r:
            unit(r)
        forward(first[r])
        across(0, r).start()


    def columns_of(n):
        for g in range(CHIP // 128):
            r, which = g // 2, g % 2
            for k in range(2):
                line = keys[n, which, k : k + 1, r * PART : (r + 1) * PART]
                columns[n, k, g * 128 : (g + 1) * 128, :] = jnp.broadcast_to(line, (128, 128)).T

    def take(n, r, follow):
        if r == 0:
            key_hop(n).wait_recv()
        hop(n, r).wait_recv()
        forward(follow)
        if r == 0:
            key_across(n).start()
        across(n, r).start()

    def cross(n, r):
        across(n, r).wait_recv()
        if r == 0:
            key_across(n).wait_recv()

    def back(n, which, target):
        return pltpu.make_async_remote_copy(
            src_ref=outbox.at[n, which], dst_ref=inbox.at[n, core], send_sem=back_send.at[n, which],
            recv_sem=back_arrive.at[n, core], device_id=target, device_id_type=MESH,
        )

    def back_wait(n, which):
        pltpu.make_async_remote_copy(
            src_ref=outbox.at[n, which], dst_ref=inbox.at[n, which], send_sem=back_send.at[n, which],
            recv_sem=back_arrive.at[n, which], device_id=sibling, device_id_type=MESH,
        ).wait_recv()

    def flush(n):
        for g in range(CHIP // 128):
            r, which = g // 2, g % 2
            best = jnp.max(col_best[n, :, g * 128 : (g + 1) * 128], axis=0, keepdims=True)
            if n in made:
                mine = row_best[n, g * 128 : (g + 1) * 128, :].T
                best = jnp.maximum(best, jnp.max(mine, axis=0, keepdims=True))
            outbox[n, which, r : r + 1, :] = best
        if n:
            for which in range(2):
                back(n, which, device(OFFSET[n], which)).start()
        else:
            back(0, other, sibling).start()

    def run(op):
        {"take": take, "cross": cross, "columns": columns_of, "flush": flush}[op[0]](*op[1:])

    bits = [jnp.int32(0), x // 2, y // 2, z // 2]

    def keep(lhs, top, rhs, col, base, score):
        lines = pl.ds(top, score.shape[0])
        cluster, rank = columns[lhs, 0, lines, :], columns[lhs, 1, lines, :]
        best = row_best[lhs, lines, :]
        for q in range(score.shape[1] // 128):
            line = pl.ds(pl.multiple_of(base // 2 + q // 2 * PART, PART), PART)
            cluster_j = keys[rhs, q % 2, 0:1, line]
            rank_j = keys[rhs, q % 2, 1:2, line]
            same = jnp.where(cluster == cluster_j, score[:, q * 128 : (q + 1) * 128], -1.0)
            later = rank > rank_j
            best = jnp.maximum(best, jnp.where(later, same, -1.0))
            back = jnp.max(jnp.where(later, -1.0, same).reshape(score.shape[0] // 8, 8, 128), axis=0)
            lanes = pl.ds(pl.multiple_of(base + q * 128, 128), 128)
            col_best[col, :, lanes] = jnp.maximum(col_best[col, :, lanes], back)
        row_best[lhs, lines, :] = best

    def product(lhs, rhs):
        return lax.dot_general(lhs, rhs, (((1,), (1,)), ((), ())), preferred_element_type=jnp.float32)

    def decode(code):
        fields = ((1, 16), (16, 16), (256, 4), (1024, 16), (16384, 4), (65536, 4))
        return (lax.rem(lax.div(code, jnp.int32(d)), jnp.int32(m)) for d, m in fields)

    def short(code):
        s, t1, r1, t2, r2, axis = decode(code)
        turn = sum((axis == k).astype(jnp.int32) * bits[k] for k in range(1, 4))
        lhs = s + turn * (t1 - s)
        todo = []
        for t, r in ((t1, r1), (t2, r2)):
            rhs, at = t + turn * (s - t), r + 2 * turn
            col = rhs + (s == t).astype(jnp.int32) * (SLOTS - rhs)
            score = product(rows[lhs].reshape(CHIP, WIDTH), rows[rhs, at].reshape(2 * PART, WIDTH))
            todo.append((rhs, col, pl.multiple_of(at * 2 * PART, 2 * PART), score))
        for rhs, col, base, score in todo:
            keep(lhs, 0, rhs, col, base, score)

    def half(code):
        s, t1, b1, t2, b2, a = decode(code)
        todo = []
        for t, b in ((t1, b1), (t2, b2)):
            score = product(
                rows[s, pl.ds(2 * a, 2)].reshape(ROWS, WIDTH), rows[t, pl.ds(2 * b, 2)].reshape(ROWS, WIDTH)
            )
            todo.append((t, pl.multiple_of(b * ROWS, ROWS), score))
        for t, base, score in todo:
            keep(s, pl.multiple_of(a * ROWS, ROWS), t, t, base, score)

    def long(code):
        s, t, *_ = decode(code)
        keep(s, 0, t, t, 0, product(rows[s].reshape(CHIP, WIDTH), rows[t].reshape(CHIP, WIDTH)))

    def encode(job):
        scale = (1, 16, 256, 1024, 16384, 65536)
        return sum(a * b for a, b in zip(job, scale))

    codes = []
    for _, _, jobs in steps:
        one, two = encode(jobs[0]), encode(jobs[1])
        codes.append(one + core * (two - one))

    def body(i, carry):
        code, wide = jnp.int32(0), jnp.int32(0)
        for k, (_, kind, _) in enumerate(steps):
            code = jnp.where(i == k, codes[k], code)
            if kind != "short":
                wide = jnp.where(i == k, ("short", "long", "half").index(kind), wide)
        for low in range(0, len(steps), GROUP):
            group = [(k, steps[k][0]) for k in range(low, min(low + GROUP, len(steps))) if steps[k][0]]

            @pl.when((i >= low) & (i < low + GROUP))
            def _(group=group):
                for k, ops in group:

                    @pl.when(i == k)
                    def _(ops=ops):
                        for op in ops:
                            run(op)

        @pl.when(wide == 0)
        def _():
            short(code)

        @pl.when(wide == 1)
        def _():
            long(code)

        @pl.when(wide == 2)
        def _():
            half(code)

        return carry

    for r in range(CHUNKS):
        cross(0, r)
    columns_of(0)
    lax.fori_loop(0, len(steps), body, 0)
    for op in rest:
        run(op)
    for n in range(SLOTS):
        for r in range(copies(n)):
            across(n, r).wait_send()
            if n:
                hop(n, r).wait_send()
        key_across(n).wait_send()
        if n:
            key_hop(n).wait_send()

    total = outbox[0, core]
    for n in range(1, SLOTS):
        for which in range(2):
            back_wait(n, which)
            total = jnp.maximum(total, inbox[n, which])
    back_wait(0, other)
    out_ref[0] = total
    out_ref[1] = inbox[0, other]
    for n in range(1, SLOTS):
        for which in range(2):
            back(n, which, sibling).wait_send()
    back(0, other, sibling).wait_send()


def local(embeddings, cluster_ids, priority):
    steps, rest, made, _ = plan()
    first = sends(steps)
    dma = pltpu.SemaphoreType.DMA
    best = pl.pallas_call(
        functools.partial(kernel, first, steps, rest, made),
        out_shape=jax.ShapeDtypeStruct((2, CHUNKS, PART), jnp.float32),
        in_specs=[pl.BlockSpec(memory_space=pl.ANY)] + [pl.BlockSpec(memory_space=pltpu.VMEM)] * 2,
        out_specs=pl.BlockSpec(memory_space=pltpu.VMEM),
        scratch_shapes=[
            pltpu.VMEM((SLOTS, CHUNKS, 2, PART, WIDTH), jnp.bfloat16),
            pltpu.VMEM((SLOTS, 2, 2, ROWS), jnp.float32),
            pltpu.VMEM((SLOTS, 2, CHIP, 128), jnp.float32),
            pltpu.VMEM((SLOTS, CHIP, 128), jnp.float32),
            pltpu.VMEM((SLOTS + 1, 8, CHIP), jnp.float32),
            pltpu.VMEM((SLOTS, 2, CHUNKS, PART), jnp.float32),
            pltpu.VMEM((SLOTS, 2, CHUNKS, PART), jnp.float32),
            dma((SLOTS, CHUNKS)),
            dma((SLOTS, CHUNKS)),
            dma((SLOTS, CHUNKS)),
            dma((SLOTS, CHUNKS)),
            dma((SLOTS,)),
            dma((SLOTS,)),
            dma((SLOTS,)),
            dma((SLOTS,)),
            dma((SLOTS, 2)),
            dma((SLOTS, 2)),
            pltpu.VMEM((ROWS, WIDTH), jnp.bfloat16),
            dma((CHUNKS,)),
        ],
        compiler_params=pltpu.CompilerParams(
            collective_id=0, has_side_effects=True, vmem_limit_bytes=60 * 2**20
        ),
    )(embeddings, cluster_ids.reshape(1, ROWS), priority.reshape(1, ROWS))
    return jnp.maximum(best[0], best[1]).reshape(ROWS)


def solution(mesh):
    placed = (P(("grp", "blk"), None), P(("grp", "blk"), None), P(("grp", "blk")))
    return jax.shard_map(
        local, mesh=mesh, in_specs=placed, out_specs=P(("grp", "blk")), check_vma=False
    )
```
